256 devices in a mesh: dp: 128 (over y, x, z_lo, core), tensor: 2 (over z_hi).
Axes of the slice: x: 4, y: 4, z: 8 (z_hi: 2, z_lo: 4; z = z_hi * 4 + z_lo), core: 2. Of those that a mesh axis runs over, the one named last changes fastest.
Arguments:
- x_in: bfloat16 [32768, 768], P('dp'), may hold values from -6 to 6
- lengths: int32 [128], P('dp'), may hold values from 51 to 256, as said below
- retrieved: int32 [32768, 1024], P('dp'), may hold values from 0 to 8191, all different within a row
- datastore: bfloat16 [8192, 768], P('dp'), may hold values from -6 to 6
- self_wq: bfloat16 [768, 768], P(None, 'tensor'), may hold values from -0.21875 to 0.21875
- self_wk: bfloat16 [768, 768], P(None, 'tensor'), may hold values from -0.21875 to 0.21875
- self_wv: bfloat16 [768, 768], P(None, 'tensor'), may hold values from -0.21875 to 0.21875
- self_wo: bfloat16 [768, 768], P('tensor'), may hold values from -1.75 to 1.75
- ln1_gain: float32 [768], replicated, may hold values from 0.1 to 1.9
- ln1_bias: float32 [768], replicated, may hold values from -3 to 3
- cross_wq: bfloat16 [768, 768], P(None, 'tensor'), may hold values from -0.3125 to 0.3125
- cross_wk: bfloat16 [768, 768], P(None, 'tensor'), may hold values from -0.21875 to 0.21875
- cross_wv: bfloat16 [768, 768], P(None, 'tensor'), may hold values from -0.21875 to 0.21875
- cross_wo: bfloat16 [768, 768], P('tensor'), may hold values from -2.5 to 2.5
- ln2_gain: float32 [768], replicated, may hold values from 0.1 to 1.9
- ln2_bias: float32 [768], replicated, may hold values from -3 to 3
- ffn_w1: bfloat16 [768, 3072], P(None, 'tensor'), may hold values from -0.21875 to 0.21875
- ffn_w2: bfloat16 [3072, 768], P('tensor'), may hold values from -0.109375 to 0.109375
- ln3_gain: float32 [768], replicated, may hold values from 0.1 to 1.9
- ln3_bias: float32 [768], replicated, may hold values from -3 to 3
- cotangent: bfloat16 [32768, 768], P('dp'), may hold values from -6 to 6
Outputs:
- block_out: bfloat16 [32768, 768], P('dp')
- input_grad: float32 [32768, 768], P('dp')
- datastore_grad: float32 [8192, 768], P('dp', 'tensor')
- self_wq_grad: float32 [768, 768], P('dp', 'tensor')
- self_wk_grad: float32 [768, 768], P('dp', 'tensor')
- self_wv_grad: float32 [768, 768], P('dp', 'tensor')
- self_wo_grad: float32 [768, 768], P('tensor', 'dp')
- ln1_gain_grad: float32 [768], P('dp')
- ln1_bias_grad: float32 [768], P('dp')
- cross_wq_grad: float32 [768, 768], P('dp', 'tensor')
- cross_wk_grad: float32 [768, 768], P('dp', 'tensor')
- cross_wv_grad: float32 [768, 768], P('dp', 'tensor')
- cross_wo_grad: float32 [768, 768], P('tensor', 'dp')
- ln2_gain_grad: float32 [768], P('dp')
- ln2_bias_grad: float32 [768], P('dp')
- ffn_w1_grad: float32 [768, 3072], P('dp', 'tensor')
- ffn_w2_grad: float32 [3072, 768], P('tensor', 'dp')
- ln3_gain_grad: float32 [768], P('dp')
- ln3_bias_grad: float32 [768], P('dp')
The draws below stay inside these ranges and needn't reach their ends.
Inputs may be any that keep to these rules, and one draw needn't show every extreme that they name: `lengths`: one sequence in every draw has all 256 slots valid. `retrieved`: each row names 1024 different datastore states.
All inputs are finite; a program needn't handle non-finite values.
Results may differ from the reference program's by a relative error of at most 0.033.
Values may be sent and summed in bfloat16 or wider, within the bound.
No kernel may reach another device: no remote copies, remote signals or barrier semaphores. Data moves between devices by JAX's collectives and lax.ppermute only.
A program may use at most 256 MiB of HBM per device.

```python
import jax
import jax.numpy as jnp
from jax import lax

D = 768
HEADS = 12
FF = 3072
HEAD_DIM = 64
TOK_DEV = 256
K_TOP = 1024
SEQS = 128
TOKENS = 32768
DATASTORE = 8192


def draw_lengths(key, part):
    key = jax.random.fold_in(key, 11)
    key_len, key_long, key_short = jax.random.split(key, 3)
    shortest = TOK_DEV // 5
    lengths_drawn = jax.random.randint(key_len, (SEQS,), shortest, TOK_DEV + 1)
    longest_at = jax.random.randint(key_long, (), 0, SEQS)
    lengths_drawn = lengths_drawn.at[longest_at].set(TOK_DEV)
    shortest_at = (longest_at + 1 + jax.random.randint(key_short, (), 0, SEQS - 1)) % SEQS
    lengths_drawn = lengths_drawn.at[shortest_at].set(shortest)
    return lengths_drawn.astype(jnp.int32)


def shard_levels(own_key, extent, cuts, least, high):
    gain = 1.0
    for axis_at, shards_of in cuts:
        draws = jax.random.uniform(jax.random.fold_in(jax.random.fold_in(own_key, 6), axis_at), (shards_of,), jnp.float32, least / len(cuts), high / len(cuts))
        gain = gain * jnp.repeat(jnp.exp(draws), extent[axis_at] // shards_of).reshape((-1,) + (1,) * (len(extent) - 1 - axis_at))
    return gain


def distinct(rng, rows, number_of, top, lift):
    order = jax.random.permutation(jax.random.fold_in(rng, 1), number_of)
    pull = order
    for power in range(3):
        pull = pull * pull // number_of
    pull = pull * lift // number_of
    chance = jax.random.randint(jax.random.fold_in(rng, 2), (rows, number_of), 0, 4096) + pull
    fixed_rows = jax.random.permutation(jax.random.fold_in(rng, 3), rows)[jnp.arange(number_of) % rows]
    chance = jnp.where(jnp.arange(rows)[:, None] == fixed_rows[None, :], 1 << 14, chance)
    priority = chance * number_of + jnp.arange(number_of)
    return lax.top_k(priority.astype(jnp.int32), top)[1].astype(jnp.int32)


def normal_values(own_key, dims, deviation, reach, cuts=(), held_as=jnp.bfloat16):
    loudness = shard_levels(own_key, dims, cuts, -0.22, 0.18) if cuts else 1.0
    result = jax.random.normal(own_key, dims, jnp.float32) * deviation * loudness
    return jnp.minimum(jnp.maximum(result, -reach), reach).astype(held_as)


def setup_inputs(seed: int = 0) -> dict:
    arg_keys = jax.random.split(jax.random.key(seed), 22)
    x_in = normal_values(arg_keys[0], (TOKENS, D), 1.0, 6.0, ((0, 128),))
    lengths = draw_lengths(jax.random.fold_in(arg_keys[21], 71), 0)
    retrieved = distinct(arg_keys[2], TOKENS, DATASTORE, K_TOP, 0)
    datastore = normal_values(arg_keys[3], (DATASTORE, D), 1.0, 6.0, ((0, 128),))
    self_wq = normal_values(arg_keys[4], (D, D), D ** -0.5, 0.21875, ((1, 2),))
    self_wk = normal_values(arg_keys[5], (D, D), D ** -0.5, 0.21875, ((1, 2),))
    self_wv = normal_values(arg_keys[6], (D, D), D ** -0.5, 0.21875, ((1, 2),))
    self_wo = normal_values(arg_keys[7], (D, D), (D // 64) ** -0.5, 1.75, ((0, 2),))
    ln1_gain = jnp.clip(1.0 + 0.18 * jax.random.normal(arg_keys[8], (D,), jnp.float32), 0.1, 1.9)
    ln1_bias = normal_values(arg_keys[9], (D,), 0.5, 3.0, (), jnp.float32)
    cross_wq = normal_values(arg_keys[10], (D, D), (D // 2) ** -0.5, 0.3125, ((1, 2),))
    cross_wk = normal_values(arg_keys[11], (D, D), D ** -0.5, 0.21875, ((1, 2),))
    cross_wv = normal_values(arg_keys[12], (D, D), D ** -0.5, 0.21875, ((1, 2),))
    cross_wo = normal_values(arg_keys[13], (D, D), (D // 128) ** -0.5, 2.5, ((0, 2),))
    ln2_gain = jnp.clip(1.0 + 0.18 * jax.random.normal(arg_keys[14], (D,), jnp.float32), 0.1, 1.9)
    ln2_bias = normal_values(arg_keys[15], (D,), 0.5, 3.0, (), jnp.float32)
    ffn_w1 = normal_values(arg_keys[16], (D, FF), D ** -0.5, 0.21875, ((1, 2),))
    ffn_w2 = normal_values(arg_keys[17], (FF, D), FF ** -0.5, 0.109375, ((0, 2),))
    ln3_gain = jnp.clip(1.0 + 0.18 * jax.random.normal(arg_keys[18], (D,), jnp.float32), 0.1, 1.9)
    ln3_bias = normal_values(arg_keys[19], (D,), 0.5, 3.0, (), jnp.float32)
    cotangent = normal_values(arg_keys[20], (TOKENS, D), 1.0, 6.0, ((0, 128),))
    return {"x_in": x_in, "lengths": lengths, "retrieved": retrieved, "datastore": datastore, "self_wq": self_wq, "self_wk": self_wk, "self_wv": self_wv, "self_wo": self_wo, "ln1_gain": ln1_gain, "ln1_bias": ln1_bias, "cross_wq": cross_wq, "cross_wk": cross_wk, "cross_wv": cross_wv, "cross_wo": cross_wo, "ln2_gain": ln2_gain, "ln2_bias": ln2_bias, "ffn_w1": ffn_w1, "ffn_w2": ffn_w2, "ln3_gain": ln3_gain, "ln3_bias": ln3_bias, "cotangent": cotangent}


@jax.custom_vjp
def low(v):
    return lax.optimization_barrier(v.astype(jnp.bfloat16)).astype(jnp.float32)

@jax.custom_vjp
def low_back(v):
    return v

def low_keep(v):
    return (low(v), None)

def low_pass(kept, grad):
    return (grad,)

def back_keep(v):
    return (v, None)

def back_low(kept, grad):
    return (low(grad),)
low.defvjp(low_keep, low_pass)
low_back.defvjp(back_keep, back_low)

def round_both(operand):
    return low_back(low(operand))

def matmul(left, right):
    return jnp.dot(left, right, precision=lax.Precision.HIGHEST)

def as_float(operand):
    return operand.astype(jnp.float32)

def layer_norm(summed, gain_vec, bias_vec):
    row_mean = lax.optimization_barrier(jnp.mean(summed, axis=-1, keepdims=True))
    centred = summed - row_mean
    variance = lax.optimization_barrier(jnp.mean(centred * centred, axis=-1, keepdims=True))
    return centred * lax.rsqrt(variance + 1e-05) * gain_vec + bias_vec

def attend(queries, key_rows, value_rows, allowed):
    scores = low_back(jnp.einsum('thd,shd->hts', queries, key_rows, precision=lax.Precision.HIGHEST)) * HEAD_DIM ** (-0.5)
    scores = jnp.where(allowed[None], scores, -1e+30)
    row_max = lax.optimization_barrier(jnp.max(scores, axis=-1, keepdims=True))
    exp_scores = jnp.exp(scores - row_max)
    attention_probs = exp_scores / lax.optimization_barrier(jnp.sum(exp_scores, axis=-1, keepdims=True))
    mixture = jnp.einsum('hts,shd->thd', low(attention_probs), value_rows, precision=lax.Precision.HIGHEST)
    return round_both(mixture.reshape(mixture.shape[0], HEADS * HEAD_DIM))

def reference(x_in, lengths, retrieved, datastore, self_wq, self_wk, self_wv, self_wo, ln1_gain, ln1_bias, cross_wq, cross_wk, cross_wv, cross_wo, ln2_gain, ln2_bias, ffn_w1, ffn_w2, ln3_gain, ln3_bias, cotangent):
    weights = tuple((as_float(matrix) for matrix in (self_wq, self_wk, self_wv, self_wo, ln1_gain, ln1_bias, cross_wq, cross_wk, cross_wv, cross_wo, ln2_gain, ln2_bias, ffn_w1, ffn_w2, ln3_gain, ln3_bias)))

    def forward(inputs, states, params):
        p_swq, p_swk, p_swv, p_swo, p_g1, p_b1, p_cwq, p_cwk, p_cwv, p_cwo, p_g2, p_b2, p_w1, p_w2, p_g3, p_b3 = params
        key_cross = round_both(matmul(states, p_cwk)).reshape(DATASTORE, HEADS, HEAD_DIM)
        value_cross = round_both(matmul(states, p_cwv)).reshape(DATASTORE, HEADS, HEAD_DIM)

        def per_sequence(carried, pieces):
            tokens_seq, length_seq, picks_seq = pieces
            positions = jnp.arange(TOK_DEV)
            query_self = round_both(matmul(tokens_seq, p_swq)).reshape(TOK_DEV, HEADS, HEAD_DIM)
            key_self = round_both(matmul(tokens_seq, p_swk)).reshape(TOK_DEV, HEADS, HEAD_DIM)
            value_self = round_both(matmul(tokens_seq, p_swv)).reshape(TOK_DEV, HEADS, HEAD_DIM)
            causal = positions[:, None] >= positions[None, :]
            mix_self = attend(query_self, key_self, value_self, causal)
            hidden_one = layer_norm(tokens_seq + low_back(matmul(mix_self, p_swo)), p_g1, p_b1)
            query_cross = round_both(matmul(low(hidden_one), p_cwq)).reshape(TOK_DEV, HEADS, HEAD_DIM)
            picked = jnp.zeros((TOK_DEV, DATASTORE), bool).at[positions[:, None], picks_seq].set(True)
            mix_cross = attend(query_cross, key_cross, value_cross, picked)
            hidden_two = layer_norm(hidden_one + low_back(matmul(mix_cross, p_cwo)), p_g2, p_b2)
            pre_act = low_back(matmul(low(hidden_two), p_w1))
            activated = low(jax.nn.gelu(pre_act))
            hidden_three = layer_norm(hidden_two + low_back(matmul(activated, p_w2)), p_g3, p_b3)
            row_valid = (positions < length_seq).astype(jnp.float32)
            return (carried, hidden_three * row_valid[:, None])
        pieces = (inputs.reshape(SEQS, TOK_DEV, D), lengths, retrieved.reshape(SEQS, TOK_DEV, K_TOP))
        unused, results = lax.scan(jax.checkpoint(per_sequence), None, pieces)
        return results.reshape(TOKENS, D)
    output, pullback = jax.vjp(forward, as_float(x_in), as_float(datastore), weights)
    grad_inputs, grad_store, grad_weights = pullback(as_float(cotangent))
    g_swq, g_swk, g_swv, g_swo, g_g1, g_b1, g_cwq, g_cwk, g_cwv, g_cwo, g_g2, g_b2, g_w1, g_w2, g_g3, g_b3 = grad_weights
    return (output.astype(jnp.bfloat16), grad_inputs, grad_store, g_swq, g_swk, g_swv, g_swo, g_g1, g_b1, g_cwq, g_cwk, g_cwv, g_cwo, g_g2, g_b2, g_w1, g_w2, g_g3, g_b3)
```

```python
import functools

import jax
import jax.numpy as jnp
from jax import lax
from jax.experimental import pallas as pl
from jax.experimental.pallas import tpu as pltpu
from jax.sharding import PartitionSpec as P

LOW = jnp.bfloat16
WIDE = jnp.float32
MASKED = -1e30
HEAD_DIM = 64
SCALE = 0.125
AXES = {"y": (4, 32), "x": (4, 8), "z": (4, 2), "core": (2, 1)}
N_DP = 128
VMEM = 48 * 2**20


def dot(left, right, left_dim=1, right_dim=0):
    return lax.dot_general(
        left, right, (((left_dim,), (right_dim,)), ((), ())), preferred_element_type=WIDE
    )


def coord(axis):
    size, stride = AXES[axis]
    return (lax.axis_index("dp") // stride) % size


def shift(value, axis, step):
    size, stride = AXES[axis]
    pairs = []
    for d in range(N_DP):
        at = (d // stride) % size
        pairs.append((d, d + ((at + step) % size - at) * stride))
    return lax.ppermute(value, "dp", pairs)


def other_tensor(value):
    return lax.ppermute(value, "tensor", [(0, 1), (1, 0)])


def tensor_total(partial_value):
    mine = partial_value.astype(LOW)
    return mine.astype(WIDE) + other_tensor(mine).astype(WIDE)


def gather(block, axis):
    return [block] + [shift(block, axis, k) for k in range(1, AXES[axis][0])]


def scatter_sum(pieces, axis):
    total = pieces[0].astype(WIDE)
    for k in range(1, len(pieces)):
        total = total + shift(pieces[k].astype(LOW), axis, -k).astype(WIDE)
    return total


def take_rows(value, index, size):
    return lax.dynamic_slice_in_dim(value, index * size, size, 0)


def weight_scatter(grads):
    n = grads.shape[1]
    half, quarter = n // 2, n // 4
    core = coord("core")
    grads = grads.astype(LOW)
    mine = lax.dynamic_slice_in_dim(grads, core * half, half, 1)
    theirs = lax.dynamic_slice_in_dim(grads, (1 - core) * half, half, 1)
    both = (mine.astype(WIDE) + shift(theirs, "core", 1).astype(WIDE)).astype(LOW)
    at_y, at_x, at_z = coord("y"), coord("x"), coord("z")
    one = both[:, :quarter]
    two = both[:, quarter:].reshape(4, 4, 48, quarter)
    one = scatter_sum([take_rows(one, (at_y - k) % 4, 192) for k in range(4)], "y")
    two = scatter_sum(
        [
            lax.dynamic_slice_in_dim(two, (at_x - k) % 4, 1, 1).reshape(192, quarter)
            for k in range(4)
        ],
        "x",
    )
    one = scatter_sum([take_rows(one, (at_x - k) % 4, 48) for k in range(4)], "x")
    two = scatter_sum([take_rows(two, (at_y - k) % 4, 48) for k in range(4)], "y")
    joined = jnp.concatenate([one, two], axis=1)
    joined = scatter_sum([take_rows(joined, (at_z - k) % 4, 12) for k in range(4)], "z")
    keep = take_rows(joined, core, 6)
    send = take_rows(joined, 1 - core, 6).astype(LOW)
    got = shift(send, "core", 1).astype(WIDE)
    first = jnp.where(core == 0, keep, got)
    second = jnp.where(core == 0, got, keep)
    return jnp.concatenate([first, second], axis=1)


def first_half_rows(pair, which):
    row = lax.broadcasted_iota(jnp.int32, pair.shape, 0)
    return jnp.where((row < HEAD_DIM) == (which == 0), pair, jnp.zeros_like(pair))


def first_half_lanes(pair, which):
    lane = lax.broadcasted_iota(jnp.int32, pair.shape, 1)
    return jnp.where((lane < HEAD_DIM) == (which == 0), pair, jnp.zeros_like(pair))


def mask_kernel(place_ref, picks_ref, out_ref, high_s, low_s, count_s):
    picks = picks_ref[...]
    core = (place_ref[3] - (picks >> 6)) & 1
    at_z = (place_ref[2] - (picks >> 7)) & 3
    at_x = (place_ref[1] - (picks >> 9)) & 3
    at_y = (place_ref[0] - (picks >> 11)) & 3
    high_s[...] = (core << 5) | (at_y << 3) | (at_x << 1) | (at_z >> 1)
    low_s[...] = ((at_z & 1) << 6) | (picks & 63)
    rows, k_top = picks_ref.shape

    def count(t, carry):
        high = high_s[pl.ds(t, 1), :]
        low = low_s[pl.ds(t, 1), :]
        is_high = lax.broadcasted_iota(jnp.int32, (64, k_top), 0) == high
        is_low = lax.broadcasted_iota(jnp.int32, (128, k_top), 0) == low
        count_s[pl.ds(pl.multiple_of(t * 64, 64), 64), :] = dot(
            jnp.where(is_high, 1.0, 0.0).astype(LOW), jnp.where(is_low, 1.0, 0.0).astype(LOW), 1, 1
        )
        return carry

    lax.fori_loop(0, rows, count, 0, unroll=4)

    def turn(h, carry):
        block = count_s[pl.ds(h, rows, stride=64), :]
        bias = jnp.where(block.T > 0.5, 0.0, MASKED)
        out_ref[pl.ds(pl.multiple_of(h * 128, 128), 128), :] = bias.astype(LOW)
        return carry

    lax.fori_loop(0, 64, turn, 0, unroll=2)


def cost(microseconds, moved):
    return pl.CostEstimate(
        flops=int(microseconds * 1e9), bytes_accessed=int(moved), transcendentals=0
    )


def retrieval_mask(place, picks):
    tokens, k_top = picks.shape
    rows = 128
    return pl.pallas_call(
        mask_kernel,
        out_shape=jax.ShapeDtypeStruct((8192, tokens), LOW),
        grid=(tokens // rows,),
        in_specs=[
            pl.BlockSpec(memory_space=pltpu.SMEM),
            pl.BlockSpec((rows, k_top), lambda i: (i, 0)),
        ],
        out_specs=pl.BlockSpec((8192, rows), lambda i: (0, i)),
        scratch_shapes=[
            pltpu.VMEM((rows, k_top), jnp.int32),
            pltpu.VMEM((rows, k_top), jnp.int32),
            pltpu.VMEM((rows * 64, 128), WIDE),
        ],
        compiler_params=pltpu.CompilerParams(vmem_limit_bytes=VMEM),
        cost_estimate=cost(43, 5e6),
        name="retrieval_mask",
    )(place, picks)


def cross_fwd_kernel(last, *refs):
    if last:
        qt_ref, k_ref, v_ref, bias_ref, acc_in, top_in, sum_in = refs[:7]
        mixt_ref, mix_ref, lse_ref, acc_s, top_s, sum_s = refs[7:]
    else:
        qt_ref, k_ref, v_ref, bias_ref = refs[:4]
        acc_s, top_s, sum_s = refs[4:]
    step = pl.program_id(0)

    @pl.when(step == 0)
    def start():
        if last:
            acc_s[...] = acc_in[...]
            top_s[...] = top_in[...]
            sum_s[...] = sum_in[...]
        else:
            acc_s[...] = jnp.zeros_like(acc_s)
            top_s[...] = jnp.full_like(top_s, MASKED)
            sum_s[...] = jnp.zeros_like(sum_s)

    bias = bias_ref[...].astype(WIDE)
    for pair in range(3):
        cols = slice(pair * 128, (pair + 1) * 128)
        keys, values, queries = k_ref[:, cols], v_ref[:, cols], qt_ref[cols, :]
        for a in range(2):
            h = 2 * pair + a
            rows = slice(h * HEAD_DIM, (h + 1) * HEAD_DIM)
            scores = dot(keys, first_half_rows(queries, a)) + bias
            old = top_s[h : h + 1, :]
            top = jnp.maximum(old, jnp.max(scores, axis=0, keepdims=True))
            fade = jnp.exp(old - top)
            weights = jnp.exp(scores - top)
            sum_s[h : h + 1, :] = sum_s[h : h + 1, :] * fade + jnp.sum(
                weights, axis=0, keepdims=True
            )
            top_s[h : h + 1, :] = top
            mixed = dot(values, weights.astype(LOW), 0, 0)
            acc_s[rows, :] = acc_s[rows, :] * fade + mixed[a * HEAD_DIM : (a + 1) * HEAD_DIM, :]

    if last:

        @pl.when(step == pl.num_programs(0) - 1)
        def finish():
            for h in range(6):
                rows = slice(h * HEAD_DIM, (h + 1) * HEAD_DIM)
                acc_s[rows, :] = acc_s[rows, :] / sum_s[h : h + 1, :]
            mixt_ref[...] = acc_s[...]
            mix_ref[...] = acc_s[...].T.astype(LOW)
            lse_ref[...] = top_s[...] + jnp.log(jnp.maximum(sum_s[...], 1e-30))


def cross_fwd(qt, keys, values, bias, offset, state=None, block=2048):
    states, tokens = keys.shape[0], qt.shape[1]
    last = state is not None
    whole = lambda i: (0, 0)
    rows = lambda i: (i, 0)
    skip = offset // block
    acc = jax.ShapeDtypeStruct((384, tokens), WIDE)
    row = jax.ShapeDtypeStruct((8, tokens), WIDE)
    state_specs = [pl.BlockSpec(a.shape, whole) for a in (acc, row, row)]
    in_specs = [
        pl.BlockSpec((384, tokens), whole),
        pl.BlockSpec((block, 384), rows),
        pl.BlockSpec((block, 384), rows),
        pl.BlockSpec((block, tokens), lambda i: (i + skip, 0)),
    ]
    scratch = []
    args = (qt, keys, values, bias)
    if last:
        in_specs += state_specs
        args += state
        out_shape = (acc, jax.ShapeDtypeStruct((tokens, 384), LOW), row)
        out_specs = [pl.BlockSpec(a.shape, whole) for a in out_shape]
        scratch = [pltpu.VMEM(a.shape, WIDE) for a in (acc, row, row)]
    else:
        out_shape, out_specs = (acc, row, row), state_specs
    return pl.pallas_call(
        functools.partial(cross_fwd_kernel, last),
        out_shape=out_shape,
        grid=(states // block,),
        in_specs=in_specs,
        out_specs=out_specs,
        scratch_shapes=scratch,
        compiler_params=pltpu.CompilerParams(vmem_limit_bytes=VMEM),
        cost_estimate=cost(15, 8e6),
        name="cross_fwd",
    )(*args)


def cross_bwd_kernel(
    qt_ref,
    q_ref,
    dmt_ref,
    dm_ref,
    lse_ref,
    inner_ref,
    dq_in,
    k_ref,
    v_ref,
    bias_ref,
    dk_ref,
    dv_ref,
    dq_ref,
):
    @pl.when(pl.program_id(0) == 0)
    def start():
        dq_ref[...] = dq_in[...]

    bias = bias_ref[...].astype(WIDE)
    for pair in range(3):
        cols = slice(pair * 128, (pair + 1) * 128)
        keys, values = k_ref[:, cols], v_ref[:, cols]
        dk = dv = None
        for a in range(2):
            h = 2 * pair + a
            rows = slice(h * HEAD_DIM, (h + 1) * HEAD_DIM)
            scores = dot(keys, first_half_rows(qt_ref[cols, :], a)) + bias
            probs = jnp.exp(scores - lse_ref[h : h + 1, :])
            dp = dot(values, first_half_rows(dmt_ref[cols, :], a))
            ds = (probs * (dp - inner_ref[h : h + 1, :])).astype(LOW)
            dv_head = dot(probs.astype(LOW), first_half_lanes(dm_ref[:, cols], a))
            dk_head = dot(ds, first_half_lanes(q_ref[:, cols], a))
            dk = dk_head if a == 0 else dk + dk_head
            dv = dv_head if a == 0 else dv + dv_head
            dq = dot(keys, ds, 0, 0)
            dq_ref[rows, :] += dq[a * HEAD_DIM : (a + 1) * HEAD_DIM, :]
        dk_ref[:, cols] = dk.astype(LOW)
        dv_ref[:, cols] = dv.astype(LOW)


def cross_bwd(qt, q, dmt, dm, lse, inner, dq, keys, values, bias, offset, block=1024):
    states, tokens = keys.shape[0], qt.shape[1]
    whole = lambda i: (0, 0)
    rows = lambda i: (i, 0)
    skip = offset // block
    return pl.pallas_call(
        cross_bwd_kernel,
        out_shape=(
            jax.ShapeDtypeStruct((states, 384), LOW),
            jax.ShapeDtypeStruct((states, 384), LOW),
            jax.ShapeDtypeStruct((384, tokens), WIDE),
        ),
        grid=(states // block,),
        in_specs=[
            pl.BlockSpec((384, tokens), whole),
            pl.BlockSpec((tokens, 384), whole),
            pl.BlockSpec((384, tokens), whole),
            pl.BlockSpec((tokens, 384), whole),
            pl.BlockSpec((8, tokens), whole),
            pl.BlockSpec((8, tokens), whole),
            pl.BlockSpec((384, tokens), whole),
            pl.BlockSpec((block, 384), rows),
            pl.BlockSpec((block, 384), rows),
            pl.BlockSpec((block, tokens), lambda i: (i + skip, 0)),
        ],
        out_specs=(
            pl.BlockSpec((block, 384), rows),
            pl.BlockSpec((block, 384), rows),
            pl.BlockSpec((384, tokens), whole),
        ),
        compiler_params=pltpu.CompilerParams(vmem_limit_bytes=VMEM),
        cost_estimate=cost(18, 14e6),
        name="cross_bwd",
    )(qt, q, dmt, dm, lse, inner, dq, keys, values, bias)


def causal_bias(tokens):
    key = lax.broadcasted_iota(jnp.int32, (tokens, tokens), 0)
    query = lax.broadcasted_iota(jnp.int32, (tokens, tokens), 1)
    return jnp.where(key <= query, 0.0, MASKED)


def self_fwd_kernel(
    x_ref, wq_ref, wk_ref, wv_ref, wo_ref, q_ref, k_ref, v_ref, mixt_ref, mix_ref, lse_ref, part_ref
):
    x = x_ref[...]
    tokens = x.shape[0]
    q_ref[...] = dot(x, wq_ref[...]).astype(LOW) * jnp.asarray(SCALE, LOW)
    k_ref[...] = dot(x, wk_ref[...]).astype(LOW)
    v_ref[...] = dot(x, wv_ref[...]).astype(LOW)
    bias = causal_bias(tokens)
    lse_ref[...] = jnp.zeros_like(lse_ref)
    for pair in range(3):
        cols = slice(pair * 128, (pair + 1) * 128)
        queries, keys, values = q_ref[:, cols], k_ref[:, cols], v_ref[:, cols]
        for a in range(2):
            h = 2 * pair + a
            scores = dot(keys, first_half_lanes(queries, a), 1, 1) + bias
            top = jnp.max(scores, axis=0, keepdims=True)
            weights = jnp.exp(scores - top)
            total = jnp.sum(weights, axis=0, keepdims=True)
            mixed = dot(values, weights.astype(LOW), 0, 0)[a * HEAD_DIM : (a + 1) * HEAD_DIM, :]
            mixt_ref[h * HEAD_DIM : (h + 1) * HEAD_DIM, :] = mixed / total
            lse_ref[h : h + 1, :] = top + jnp.log(total)
    mix_ref[...] = mixt_ref[...].T.astype(LOW)
    part_ref[...] = dot(mix_ref[...], wo_ref[...]).astype(LOW)


def self_fwd(x, wq, wk, wv, wo):
    tokens = x.shape[0]
    narrow = jax.ShapeDtypeStruct((tokens, 384), LOW)
    return pl.pallas_call(
        self_fwd_kernel,
        out_shape=(
            narrow,
            narrow,
            narrow,
            jax.ShapeDtypeStruct((384, tokens), WIDE),
            narrow,
            jax.ShapeDtypeStruct((8, tokens), WIDE),
            jax.ShapeDtypeStruct((tokens, 768), LOW),
        ),
        compiler_params=pltpu.CompilerParams(vmem_limit_bytes=VMEM),
        cost_estimate=cost(8, 4e6),
        name="self_fwd",
    )(x, wq, wk, wv, wo)


def self_bwd_kernel(
    e_ref,
    q_ref,
    k_ref,
    v_ref,
    mixt_ref,
    lse_ref,
    wq_ref,
    wk_ref,
    wv_ref,
    wo_ref,
    dq_ref,
    dk_ref,
    dv_ref,
    part_ref,
    dqt_s,
):
    tokens = e_ref.shape[0]
    dm = dot(e_ref[...], wo_ref[...], 1, 1).astype(LOW)
    dmt = dm.astype(WIDE).T
    bias = causal_bias(tokens)
    for pair in range(3):
        cols = slice(pair * 128, (pair + 1) * 128)
        queries, keys, values, dm_pair = q_ref[:, cols], k_ref[:, cols], v_ref[:, cols], dm[:, cols]
        dk = dv = None
        for a in range(2):
            h = 2 * pair + a
            rows = slice(h * HEAD_DIM, (h + 1) * HEAD_DIM)
            q_head = first_half_lanes(queries, a)
            dm_head = first_half_lanes(dm_pair, a)
            inner = jnp.sum(dmt[rows, :] * mixt_ref[rows, :], axis=0, keepdims=True)
            scores = dot(keys, q_head, 1, 1) + bias
            probs = jnp.exp(scores - lse_ref[h : h + 1, :])
            dp = dot(values, dm_head, 1, 1)
            ds = (probs * (dp - inner)).astype(LOW)
            dv_head = dot(probs.astype(LOW), dm_head)
            dk_head = dot(ds, q_head)
            dk = dk_head if a == 0 else dk + dk_head
            dv = dv_head if a == 0 else dv + dv_head
            dqt_s[rows, :] = dot(keys, ds, 0, 0)[a * HEAD_DIM : (a + 1) * HEAD_DIM, :] * SCALE
        dk_ref[:, cols] = dk.astype(LOW)
        dv_ref[:, cols] = dv.astype(LOW)
    dq_ref[...] = dqt_s[...].T.astype(LOW)
    part_ref[...] = (
        dot(dq_ref[...], wq_ref[...], 1, 1)
        + dot(dk_ref[...], wk_ref[...], 1, 1)
        + dot(dv_ref[...], wv_ref[...], 1, 1)
    ).astype(LOW)


def self_bwd(e_one, q, k, v, mixt, lse, wq, wk, wv, wo):
    tokens = e_one.shape[0]
    narrow = jax.ShapeDtypeStruct((tokens, 384), LOW)
    return pl.pallas_call(
        self_bwd_kernel,
        out_shape=(narrow, narrow, narrow, jax.ShapeDtypeStruct((tokens, 768), LOW)),
        scratch_shapes=[pltpu.VMEM((384, tokens), WIDE)],
        compiler_params=pltpu.CompilerParams(vmem_limit_bytes=VMEM),
        cost_estimate=cost(10, 5e6),
        name="self_bwd",
    )(e_one, q, k, v, mixt, lse, wq, wk, wv, wo)


def layer_norm(summed, gain_vec, bias_vec):
    row_mean = jnp.mean(summed, axis=-1, keepdims=True)
    centred = summed - row_mean
    variance = jnp.mean(centred * centred, axis=-1, keepdims=True)
    inv_std = lax.rsqrt(variance + 1e-05)
    normed = centred * inv_std
    return (normed * gain_vec + bias_vec, normed, inv_std)


def norm_back(grad_out, normed, inv_std, gain_vec):
    grad_normed = grad_out * gain_vec
    centre_term = jnp.mean(grad_normed, axis=-1, keepdims=True)
    slope_term = jnp.mean(grad_normed * normed, axis=-1, keepdims=True)
    grad_in = inv_std * (grad_normed - centre_term - normed * slope_term)
    return (grad_in, jnp.sum(grad_out * normed, axis=0), jnp.sum(grad_out, axis=0))


def shards(
    x_in,
    lengths,
    retrieved,
    datastore,
    self_wq,
    self_wk,
    self_wv,
    self_wo,
    ln1_gain,
    ln1_bias,
    cross_wq,
    cross_wk,
    cross_wv,
    cross_wo,
    ln2_gain,
    ln2_bias,
    ffn_w1,
    ffn_w2,
    ln3_gain,
    ln3_bias,
    cotangent,
):
    tokens = x_in.shape[0]
    positions = lax.iota(jnp.int32, tokens)

    k_own = dot(datastore, cross_wk).astype(LOW)
    v_own = dot(datastore, cross_wv).astype(LOW)
    for axis in ("z", "x", "y"):
        k_own = jnp.concatenate(gather(k_own, axis), axis=0)
    v_own = jnp.concatenate(gather(v_own, "z"), axis=0)
    v_own = jnp.concatenate(gather(v_own, "y"), axis=0).reshape(4, 1, 256, 384)
    v_own = jnp.concatenate(gather(v_own, "x"), axis=1).reshape(4096, 384)
    k_far, v_far = shift(k_own, "core", 1), shift(v_own, "core", 1)

    q_self, k_self, v_self, mixt_self, mix_self, lse_self, part = self_fwd(
        x_in, self_wq, self_wk, self_wv, self_wo
    )
    place = jnp.stack([coord("y"), coord("x"), coord("z"), coord("core")]).astype(jnp.int32)
    bias = retrieval_mask(place, retrieved)
    h_one, normed_one, inv_one = layer_norm(
        x_in.astype(WIDE) + tensor_total(part), ln1_gain, ln1_bias
    )
    h_one_low = h_one.astype(LOW)
    q_cross = dot(h_one_low, cross_wq).astype(LOW) * jnp.asarray(SCALE, LOW)
    qt_cross = q_cross.T
    state = cross_fwd(qt_cross, k_own, v_own, bias, 0)
    mixt_cross, mix_cross, lse_cross = cross_fwd(qt_cross, k_far, v_far, bias, 4096, tuple(state))
    h_two, normed_two, inv_two = layer_norm(
        h_one + tensor_total(dot(mix_cross, cross_wo)), ln2_gain, ln2_bias
    )
    h_two_low = h_two.astype(LOW)
    pre_act = dot(h_two_low, ffn_w1)
    act_low = jax.nn.gelu(pre_act).astype(LOW)
    h_three, normed_three, inv_three = layer_norm(
        h_two + tensor_total(dot(act_low, ffn_w2)), ln3_gain, ln3_bias
    )
    row_valid = (positions < lengths[0]).astype(WIDE)[:, None]
    block_out = (h_three * row_valid).astype(LOW)

    grad_out = cotangent.astype(WIDE) * row_valid
    d_three, grad_g3, grad_b3 = norm_back(grad_out, normed_three, inv_three, ln3_gain)
    e_three = d_three.astype(LOW)
    d_act = dot(e_three, ffn_w2, 1, 1)
    unused, gelu_back = jax.vjp(jax.nn.gelu, pre_act)
    d_pre = gelu_back(d_act)[0].astype(LOW)
    d_h_two = d_three + tensor_total(dot(d_pre, ffn_w1, 1, 1))
    grads_ffn = jnp.concatenate(
        [dot(h_two_low, d_pre, 0, 0).astype(LOW), dot(e_three, act_low, 0, 0).astype(LOW)], axis=1
    )
    d_two, grad_g2, grad_b2 = norm_back(d_h_two, normed_two, inv_two, ln2_gain)
    e_two = d_two.astype(LOW)
    dm_cross = dot(e_two, cross_wo, 1, 1).astype(LOW)
    dmt_cross = dm_cross.T
    inner = jnp.sum((dmt_cross.astype(WIDE) * mixt_cross).reshape(6, HEAD_DIM, tokens), axis=1)
    inner = jnp.concatenate([inner, jnp.zeros((2, tokens), WIDE)], axis=0)
    sides = (qt_cross, q_cross, dmt_cross, dm_cross, lse_cross, inner)
    dk_far, dv_far, dqt = cross_bwd(
        *sides, jnp.zeros((384, tokens), WIDE), k_far, v_far, bias, 4096
    )
    dk_got, dv_got = shift(dk_far, "core", 1), shift(dv_far, "core", 1)
    dk_own, dv_own, dqt = cross_bwd(*sides, dqt, k_own, v_own, bias, 0)
    dqt_low = (dqt * SCALE).astype(LOW)
    d_h_one = d_two + tensor_total(dot(dqt_low, cross_wq, 0, 1))

    ffn_sum = weight_scatter(grads_ffn)

    dk = (dk_own.astype(WIDE) + dk_got.astype(WIDE)).astype(LOW)
    dv = (dv_own.astype(WIDE) + dv_got.astype(WIDE)).astype(LOW)
    dk = scatter_sum([dk[k * 1024 : (k + 1) * 1024] for k in range(4)], "y")
    dv = dv.reshape(4, 4, 256, 384)
    dv = scatter_sum([dv[:, k].reshape(1024, 384) for k in range(4)], "x")
    dk = scatter_sum([dk[k * 256 : (k + 1) * 256] for k in range(4)], "x")
    dv = scatter_sum([dv[k * 256 : (k + 1) * 256] for k in range(4)], "y")
    dk_low = scatter_sum([dk[k * 64 : (k + 1) * 64] for k in range(4)], "z").astype(LOW)
    dv_low = scatter_sum([dv[k * 64 : (k + 1) * 64] for k in range(4)], "z").astype(LOW)
    store_part = dot(dk_low, cross_wk, 1, 1) + dot(dv_low, cross_wv, 1, 1)
    tensor_at = lax.axis_index("tensor")
    store_mine = lax.dynamic_slice_in_dim(store_part, tensor_at * 384, 384, 1)
    store_send = lax.dynamic_slice_in_dim(store_part, (1 - tensor_at) * 384, 384, 1)
    datastore_grad = store_mine + other_tensor(store_send.astype(LOW)).astype(WIDE)
    store_sum = weight_scatter(
        jnp.concatenate([dot(datastore, dk_low, 0, 0), dot(datastore, dv_low, 0, 0)], axis=1)
    )

    d_one, grad_g1, grad_b1 = norm_back(d_h_one, normed_one, inv_one, ln1_gain)
    e_one = d_one.astype(LOW)
    dq_self, dk_self, dv_self, part = self_bwd(
        e_one,
        q_self,
        k_self,
        v_self,
        mixt_self,
        lse_self,
        self_wq,
        self_wk,
        self_wv,
        self_wo,
    )
    input_grad = d_one + tensor_total(part)
    vectors = jnp.stack([grad_g1, grad_b1, grad_g2, grad_b2, grad_g3, grad_b3], axis=1)
    grads = [
        dot(x_in, dq_self, 0, 0),
        dot(x_in, dk_self, 0, 0),
        dot(x_in, dv_self, 0, 0),
        dot(e_one, mix_self, 0, 0),
        dot(h_one_low, dqt_low, 0, 1),
        dot(e_two, mix_cross, 0, 0),
        jnp.pad(vectors, ((0, 0), (0, 250))),
    ]
    late_sum = weight_scatter(jnp.concatenate([g.astype(LOW) for g in grads], axis=1))
    part_of = lambda k: late_sum[:, k * 384 : (k + 1) * 384]
    vector = lambda k: late_sum[:, 2304 + k]
    return (
        block_out,
        input_grad,
        datastore_grad,
        part_of(0),
        part_of(1),
        part_of(2),
        part_of(3).T,
        vector(0),
        vector(1),
        part_of(4),
        store_sum[:, :384],
        store_sum[:, 384:],
        part_of(5).T,
        vector(2),
        vector(3),
        ffn_sum[:, :1536],
        ffn_sum[:, 1536:].T,
        vector(4),
        vector(5),
    )


def solution(mesh):
    rows, columns, split = P("dp", None), P(None, "tensor"), P("tensor", None)
    norm = (P(), P())
    in_specs = (
        (rows, P("dp"), rows, rows)
        + (columns, columns, columns, split)
        + norm
        + (columns, columns, columns, split)
        + norm
        + (columns, split)
        + norm
        + (rows,)
    )
    both, turned, vector = P("dp", "tensor"), P("tensor", "dp"), P("dp")
    out_specs = (
        (rows, rows, both)
        + (both, both, both, turned)
        + (vector, vector)
        + (both, both, both, turned)
        + (vector, vector)
        + (both, turned)
        + (vector, vector)
    )
    return jax.shard_map(shards, mesh=mesh, in_specs=in_specs, out_specs=out_specs, check_vma=False)
```

```python
import functools

import jax
import jax.numpy as jnp
from jax import lax
from jax.experimental import pallas as pl
from jax.experimental.pallas import tpu as pltpu
from jax.sharding import PartitionSpec as P

LOW = jnp.bfloat16
WIDE = jnp.float32
MASKED = -1e30
HEAD_DIM = 64
SCALE = 0.125
AXES = {"y": (4, 32), "x": (4, 8), "z": (4, 2), "core": (2, 1)}
N_DP = 128
VMEM = 32 * 2**20


def dot(left, right, left_dim=1, right_dim=0):
    return lax.dot_general(
        left, right, (((left_dim,), (right_dim,)), ((), ())), preferred_element_type=WIDE
    )


def coord(axis):
    size, stride = AXES[axis]
    return (lax.axis_index("dp") // stride) % size


def shift(value, axis, step):
    size, stride = AXES[axis]
    pairs = []
    for d in range(N_DP):
        at = (d // stride) % size
        pairs.append((d, d + ((at + step) % size - at) * stride))
    return lax.ppermute(value, "dp", pairs)


def other_tensor(value):
    return lax.ppermute(value, "tensor", [(0, 1), (1, 0)])


def tensor_total(partial_value):
    mine = partial_value.astype(LOW)
    return mine.astype(WIDE) + other_tensor(mine).astype(WIDE)


def shifts(value, axis):
    return [shift(value, axis, k) for k in range(1, AXES[axis][0])]


def returns(pieces, axis):
    return [shift(piece, axis, -1 - k) for k, piece in enumerate(pieces)]


def neighbours(block, axis):
    one, three = shift(block, axis, 1), shift(block, axis, -1)
    return one, three


def whole_kernel(body, out_shape, args, name, microseconds, scratch=(), scalars=0, after=()):
    spec = lambda a: pl.BlockSpec(a.shape, lambda i: (0,) * len(a.shape))
    in_specs = [pl.BlockSpec(memory_space=pltpu.SMEM)] * scalars
    in_specs += [spec(a) for a in args[scalars:]]
    in_specs += [pl.BlockSpec(memory_space=pl.ANY)] * len(after)
    out_specs = [spec(a) for a in out_shape] if isinstance(out_shape, list) else spec(out_shape)
    used, skipped = len(args), len(args) + len(after)

    def kernel(*refs):
        body(*refs[:used], *refs[skipped:])

    return pl.pallas_call(
        kernel,
        out_shape=out_shape,
        grid=(1,),
        in_specs=in_specs,
        out_specs=out_specs,
        scratch_shapes=list(scratch),
        compiler_params=pltpu.CompilerParams(vmem_limit_bytes=VMEM),
        cost_estimate=cost(microseconds, 1e6),
        name=name,
    )(*args, *after)


def cost(microseconds, moved):
    return pl.CostEstimate(
        flops=int(microseconds * 5e9), bytes_accessed=int(moved), transcendentals=0
    )


def low_array(*shape):
    return jax.ShapeDtypeStruct(shape, LOW)


def wide_array(*shape):
    return jax.ShapeDtypeStruct(shape, WIDE)


def first_half_rows(pair, which):
    row = lax.broadcasted_iota(jnp.int32, pair.shape, 0)
    return jnp.where((row < HEAD_DIM) == (which == 0), pair, jnp.zeros_like(pair))


def first_half_lanes(pair, which):
    lane = lax.broadcasted_iota(jnp.int32, pair.shape, 1)
    return jnp.where((lane < HEAD_DIM) == (which == 0), pair, jnp.zeros_like(pair))


def project_store(datastore, wk, wv):
    def body(s_ref, k_ref, v_ref, out_ref):
        out_ref[:, :384] = dot(s_ref[...], k_ref[...]).astype(LOW)
        out_ref[:, 384:768] = dot(s_ref[...], v_ref[...]).astype(LOW)
        out_ref[:, 768:] = s_ref[...]

    return whole_kernel(body, low_array(64, 1536), (datastore, wk, wv), "project_store", 1)


def join_near(pieces, after):
    def body(*refs):
        for k in range(4):
            refs[4][k * 32 : (k + 1) * 32, :] = refs[k][:32, :]
            refs[5][k * 32 : (k + 1) * 32, :] = refs[k][32:, :]

    return whole_kernel(body, [low_array(128, 1536)] * 2, pieces, "join_near", 1, after=after)


def halve(one_a, three_a, one_b, three_b, after):
    rows, width = one_a.shape
    half = rows // 2

    def body(*refs):
        for k in range(4):
            refs[4 + k][...] = refs[k][:half, :] if k % 2 == 0 else refs[k][half:, :]

    return whole_kernel(
        body, [low_array(half, width)] * 4, (one_a, three_a, one_b, three_b), "halve", 1, after=after
    )


def pass_on(halves, axis_a, axis_b):
    low_a, high_a, low_b, high_b = halves
    return (
        shift(low_a, axis_a, 1),
        shift(high_a, axis_a, -1),
        shift(low_b, axis_b, 1),
        shift(high_b, axis_b, -1),
    )


def join_four(pieces_a, pieces_b, after):
    def body(*refs):
        ins, outs = refs[:10], refs[10:]
        for g in range(2):
            own, one, three, low, high = ins[5 * g : 5 * g + 5]
            for ref, at in ((own, 0), (one, 128), (low, 256), (high, 320), (three, 384)):
                rows = slice(at, at + ref.shape[0])
                outs[g][rows, :] = ref[:, :768]
                outs[2][g * 512 + at : g * 512 + at + ref.shape[0], :] = ref[:, :768]
                outs[3 + g][rows, :] = ref[:, 768:]

    out_shape = [low_array(512, 768)] * 2 + [low_array(1024, 768)] + [low_array(512, 768)] * 2
    return whole_kernel(body, out_shape, (*pieces_a, *pieces_b), "join_four", 2, after=after)


def mask_body(place_ref, picks_ref, out_ref, high_s, low_s, count_s):
    picks = picks_ref[...]
    core = (place_ref[3] - (picks >> 6)) & 1
    at_z = (place_ref[2] - (picks >> 7)) & 3
    at_x = (place_ref[1] - (picks >> 9)) & 3
    at_y = (place_ref[0] - (picks >> 11)) & 3
    group = (picks >> 5) & 1
    chunk = jnp.where(group == 0, at_y, at_x)
    inside = jnp.where(group == 0, at_x, at_y)
    high_s[...] = (core << 5) | (chunk << 3) | (group << 2) | inside
    low_s[...] = (at_z << 5) | (picks & 31)
    rows, k_top = picks_ref.shape

    def count(t, carry):
        high = high_s[pl.ds(t, 1), :]
        low = low_s[pl.ds(t, 1), :]
        is_high = lax.broadcasted_iota(jnp.int32, (64, k_top), 0) == high
        is_low = lax.broadcasted_iota(jnp.int32, (128, k_top), 0) == low
        count_s[pl.ds(pl.multiple_of(t * 64, 64), 64), :] = dot(
            jnp.where(is_high, 1.0, 0.0).astype(jnp.float8_e4m3fn),
            jnp.where(is_low, 1.0, 0.0).astype(jnp.float8_e4m3fn),
            1,
            1,
        )
        return carry

    lax.fori_loop(0, rows, count, 0, unroll=8)

    def turn(h, carry):
        block = count_s[pl.ds(h, rows, stride=64), :]
        bias = jnp.where(block.T > 0.5, 0.0, MASKED)
        out_ref[pl.ds(pl.multiple_of(h * 128, 128), 128), :] = bias.astype(LOW)
        return carry

    lax.fori_loop(0, 64, turn, 0, unroll=2)


def retrieval_mask(place, picks, part, after):
    tokens, k_top = picks.shape
    rows = tokens // 2

    def kernel(place_ref, picks_ref, *refs):
        mask_body(place_ref, picks_ref, *refs[len(after) :])

    return pl.pallas_call(
        kernel,
        out_shape=low_array(8192, rows),
        grid=(1,),
        in_specs=[
            pl.BlockSpec(memory_space=pltpu.SMEM),
            pl.BlockSpec((rows, k_top), lambda i: (part, 0)),
        ]
        + anywhere(len(after)),
        out_specs=pl.BlockSpec((8192, rows), lambda i: (0, 0)),
        scratch_shapes=[
            pltpu.VMEM((rows, k_top), jnp.int32),
            pltpu.VMEM((rows, k_top), jnp.int32),
            pltpu.VMEM((rows * 64, 128), WIDE),
        ],
        compiler_params=pltpu.CompilerParams(vmem_limit_bytes=VMEM),
        cost_estimate=cost(17, 3e6),
        name="retrieval_mask",
    )(place, picks, *after)


def load_blocks(blocks, refs, into, sems, column):
    for i, pieces in enumerate(blocks):
        for operand, row, rows, to in pieces:
            pltpu.make_async_copy(
                refs[operand].at[pl.ds(row, rows)],
                into.at[i, pl.ds(to, rows)],
                sems.at[i, column],
            ).start()

    def wait(i):
        pltpu.make_async_copy(into.at[i], into.at[i], sems.at[i, column]).wait()

    return wait


def load_masks(chunks, bias_refs, into, sems, column):
    for i, chunk in enumerate(chunks):
        for j in range(2):
            pltpu.make_async_copy(
                bias_refs[j].at[pl.ds(chunk * 1024, 1024)],
                into.at[i, :, pl.ds(j * 128, 128)],
                sems.at[i, column],
            ).start()

    def wait(i):
        pltpu.make_async_copy(into.at[i], into.at[i], sems.at[i, column]).wait()

    return wait


def in_vmem(count):
    return [pl.BlockSpec(memory_space=pltpu.VMEM)] * count


def anywhere(count):
    return [pl.BlockSpec(memory_space=pl.ANY)] * count


def cross_fwd_body(chunks, blocks, counts, first, last, collect, *refs):
    n = len(chunks)
    n_arrays, n_after = counts
    qt_ref, refs = refs[0], refs[1:]
    if not first:
        state, refs = refs[:3], refs[3:]
    bias_refs, arrays, refs = refs[:2], refs[2 : 2 + n_arrays], refs[2 + n_arrays + n_after :]
    outs, refs = refs[:3], refs[3:]
    if collect:
        collected, refs = refs[0], refs[1:]
    kv_s, bias_s, sems, out_sem = refs[:4]
    if last:
        mixt_ref, mix_ref, lse_ref = outs
        acc, top_s, sum_s = refs[4:]
    else:
        acc, top_s, sum_s = outs
    wait_kv = load_blocks(blocks, arrays, kv_s, sems, 0)
    wait_bias = load_masks(chunks, bias_refs, bias_s, sems, 1)
    if first:
        acc[...] = jnp.zeros_like(acc)
        top_s[...] = jnp.full_like(top_s, MASKED)
        sum_s[...] = jnp.zeros_like(sum_s)
    else:
        acc[...] = state[0][...]
        top_s[...] = state[1][...]
        sum_s[...] = state[2][...]

    def step(i, carry):
        wait_kv(i)
        if collect:
            rows = pl.ds(pl.multiple_of(i * 1024, 1024), 1024)
            pltpu.make_async_copy(kv_s.at[i], collected.at[rows], out_sem).start()
        wait_bias(i)
        bias = bias_s[i].astype(WIDE)
        for pair in range(3):
            cols = slice(pair * 128, (pair + 1) * 128)
            keys = kv_s[i, :, cols]
            values = kv_s[i, :, 384 + pair * 128 : 512 + pair * 128]
            queries = qt_ref[cols, :]
            for a in range(2):
                h = 2 * pair + a
                rows = slice(h * HEAD_DIM, (h + 1) * HEAD_DIM)
                scores = dot(keys, first_half_rows(queries, a)) + bias
                old = top_s[h : h + 1, :]
                top = jnp.maximum(old, jnp.max(scores, axis=0, keepdims=True))
                fade = jnp.exp(old - top)
                weights = jnp.exp(scores - top)
                sum_s[h : h + 1, :] = sum_s[h : h + 1, :] * fade + jnp.sum(
                    weights, axis=0, keepdims=True
                )
                top_s[h : h + 1, :] = top
                mixed = dot(values, weights.astype(LOW), 0, 0)
                acc[rows, :] = acc[rows, :] * fade + mixed[a * HEAD_DIM : (a + 1) * HEAD_DIM, :]
        return carry

    lax.fori_loop(0, n, step, 0)
    if last:
        for h in range(6):
            rows = slice(h * HEAD_DIM, (h + 1) * HEAD_DIM)
            acc[rows, :] = acc[rows, :] / sum_s[h : h + 1, :]
        mixt_ref[...] = acc[...]
        mix_ref[...] = acc[...].T.astype(LOW)
        lse_ref[...] = top_s[...] + jnp.log(jnp.maximum(sum_s[...], 1e-30))
    if collect:
        pltpu.make_async_copy(collected, collected, out_sem).wait()


def cross_fwd(
    qt, bias, chunks, blocks, arrays, state=None, last=False, collect=False, after=()
):
    tokens, n = qt.shape[1], len(chunks)
    kept = [wide_array(384, tokens), wide_array(8, tokens), wide_array(8, tokens)]
    scratch = [
        pltpu.VMEM((n, 1024, 768), LOW),
        pltpu.VMEM((n, 1024, tokens), LOW),
        pltpu.SemaphoreType.DMA((n, 2)),
        pltpu.SemaphoreType.DMA,
    ]
    if last:
        out_shape = [kept[0], low_array(tokens, 384), kept[1]]
        scratch += [pltpu.VMEM(a.shape, WIDE) for a in kept]
    else:
        out_shape = list(kept)
    out_specs = in_vmem(3)
    if collect:
        out_shape.append(low_array(n * 1024, 768))
        out_specs += anywhere(1)
    given = (qt,) + (() if state is None else tuple(state))
    return pl.pallas_call(
        functools.partial(
            cross_fwd_body,
            chunks,
            blocks,
            (len(arrays), len(after)),
            state is None,
            last,
            collect,
        ),
        out_shape=out_shape,
        in_specs=in_vmem(len(given)) + anywhere(2 + len(arrays) + len(after)),
        out_specs=out_specs,
        scratch_shapes=scratch,
        compiler_params=pltpu.CompilerParams(vmem_limit_bytes=VMEM),
        cost_estimate=cost(4 * n, 2e6 * n),
        name="cross_fwd",
    )(*given, *bias, *arrays, *after)


def cross_bwd_body(chunks, blocks, adds, halves, pieces, counts, *refs):
    n = len(chunks)
    n_arrays, n_adds, n_halves, n_after = counts
    qt_ref, q_ref, dmt_ref, dm_ref, lse_ref, inner_ref, dq_in = refs[:7]
    bias_refs, refs = refs[7:9], refs[9:]
    arrays, refs = refs[:n_arrays], refs[n_arrays:]
    add_refs, refs = refs[:n_adds], refs[n_adds:]
    half_refs, refs = refs[:n_halves], refs[n_halves + n_after :]
    dq_ref, outs, refs = refs[0], refs[1 : 1 + len(pieces)], refs[1 + len(pieces) :]
    kv_s, bias_s, out_s, sems, out_sems, refs = *refs[:5], refs[5:]
    wait_kv = load_blocks(blocks, arrays, kv_s, sems, 0)
    wait_bias = load_masks(chunks, bias_refs, bias_s, sems, 1)
    if adds:
        add_s = refs[0]
        wait_add = load_blocks(adds, add_refs, add_s, sems, 2)
    if halves:
        half_s = refs[1]
        wait_half = load_blocks(halves, half_refs, half_s, sems, 3)
        for i in range(n):
            wait_add(i)
            wait_half(i)
            for g in range(2):
                at = slice(g * 512 + i * 256, g * 512 + i * 256 + 256)
                both = add_s[i, at, :].astype(WIDE) + half_s[i, g * 256 : g * 256 + 256, :].astype(
                    WIDE
                )
                add_s[i, at, :] = both.astype(LOW)
    dq_ref[...] = dq_in[...]

    def step(i, carry):
        wait_kv(i)
        wait_bias(i)
        if adds and not halves:
            wait_add(i)
        bias = bias_s[i].astype(WIDE)
        for pair in range(3):
            cols = slice(pair * 128, (pair + 1) * 128)
            v_cols = slice(384 + pair * 128, 512 + pair * 128)
            keys, values = kv_s[i, :, cols], kv_s[i, :, v_cols]
            dk = dv = None
            for a in range(2):
                h = 2 * pair + a
                rows = slice(h * HEAD_DIM, (h + 1) * HEAD_DIM)
                scores = dot(keys, first_half_rows(qt_ref[cols, :], a)) + bias
                probs = jnp.exp(scores - lse_ref[h : h + 1, :])
                dp = dot(values, first_half_rows(dmt_ref[cols, :], a))
                ds = (probs * (dp - inner_ref[h : h + 1, :])).astype(LOW)
                dv_head = dot(probs.astype(LOW), first_half_lanes(dm_ref[:, cols], a))
                dk_head = dot(ds, first_half_lanes(q_ref[:, cols], a))
                dk = dk_head if a == 0 else dk + dk_head
                dv = dv_head if a == 0 else dv + dv_head
                dq = dot(keys, ds, 0, 0)
                dq_ref[rows, :] += dq[a * HEAD_DIM : (a + 1) * HEAD_DIM, :]
            if adds:
                dk = dk + add_s[i, :, cols].astype(WIDE)
                dv = dv + add_s[i, :, v_cols].astype(WIDE)
            out_s[i, :, cols] = dk.astype(LOW)
            out_s[i, :, v_cols] = dv.astype(LOW)
        return carry

    if n == 1:
        step(0, 0)
    else:
        lax.fori_loop(0, n, step, 0)
    copies = []
    for j, (i, row, rows) in enumerate(pieces):
        if rows > 1024:
            for b in range(n):
                copies.append(
                    pltpu.make_async_copy(
                        out_s.at[b], outs[j].at[pl.ds(b * 1024, 1024)], out_sems.at[b]
                    )
                )
        else:
            copies.append(
                pltpu.make_async_copy(out_s.at[i, pl.ds(row, rows)], outs[j], out_sems.at[j])
            )
    for copy in copies:
        copy.start()
    for copy in copies:
        copy.wait()


def cross_bwd(
    sides, dq, bias, chunks, blocks, arrays, pieces, adds=(), add_arrays=(), halves=(),
    half_arrays=(), after=(),
):
    tokens, n = dq.shape[1], len(chunks)
    scratch = [
        pltpu.VMEM((n, 1024, 768), LOW),
        pltpu.VMEM((n, 1024, tokens), LOW),
        pltpu.VMEM((n, 1024, 768), LOW),
        pltpu.SemaphoreType.DMA((n, 4)),
        pltpu.SemaphoreType.DMA((max(n, len(pieces)),)),
    ]
    if adds:
        scratch.append(pltpu.VMEM((n, 1024, 768), LOW))
    if halves:
        scratch.append(pltpu.VMEM((n, 512, 768), LOW))
    counts = (len(arrays), len(add_arrays), len(half_arrays), len(after))
    return pl.pallas_call(
        functools.partial(cross_bwd_body, chunks, blocks, adds, halves, pieces, counts),
        out_shape=[wide_array(384, tokens)] + [low_array(rows, 768) for _, _, rows in pieces],
        in_specs=in_vmem(7) + anywhere(2 + sum(counts)),
        out_specs=in_vmem(1) + anywhere(len(pieces)),
        scratch_shapes=scratch,
        compiler_params=pltpu.CompilerParams(vmem_limit_bytes=VMEM),
        cost_estimate=cost(4.5 * n, 4e6 * n),
        name="cross_bwd",
    )(*sides, dq, *bias, *arrays, *add_arrays, *half_arrays, *after)


def store_sum_far(own, got):
    def body(*refs):
        ins, outs = refs[:6], refs[6:]
        for g in range(2):
            total = ins[g][...].astype(WIDE)
            for k in range(2):
                total = total + ins[2 + 2 * g + k][...].astype(WIDE)
            for k in range(4):
                outs[4 * g + k][...] = total[k * 128 : (k + 1) * 128, :].astype(LOW)

    return whole_kernel(
        body, [low_array(128, 768)] * 8, (*own, *got[0], *got[1]), "store_sum_far", 2
    )


def store_weight_grads(place, states, blocks):
    def body(place_ref, *refs):
        sum_s = refs[12]
        for c in range(0, 768, 256):
            total = None
            for g in range(2):
                for k in range(4):
                    part = dot(
                        refs[g][k * 128 : (k + 1) * 128, c : c + 256], refs[2 + 4 * g + k][...], 0, 0
                    )
                    total = part if total is None else total + part
            sum_s[c : c + 256, :] = total.astype(LOW)
        mine = pl.multiple_of(place_ref[3] * 384, 128)
        theirs = pl.multiple_of((1 - place_ref[3]) * 384, 128)
        refs[10][...] = sum_s[:, pl.ds(mine, 384)]
        refs[11][...] = sum_s[:, pl.ds(theirs, 384)]

    return whole_kernel(
        body,
        [low_array(768, 384)] * 2,
        (place, *states, *blocks),
        "store_weight_grads",
        3,
        scratch=[pltpu.VMEM((768, 768), LOW)],
        scalars=1,
    )


def store_sum_mid(own, got):
    def body(*refs):
        ins, outs = refs[:8], refs[8:]
        for g in range(2):
            total = ins[g][...].astype(WIDE)
            for k in range(3):
                total = total + ins[2 + 3 * g + k][...].astype(WIDE)
            for k in range(4):
                outs[k][g * 32 : (g + 1) * 32, :] = total[k * 32 : (k + 1) * 32, :].astype(LOW)

    return whole_kernel(body, [low_array(64, 768)] * 4, (*own, *got[0], *got[1]), "store_sum_mid", 1)


def store_finish(tensor_at, pieces, wk, wv):
    def body(at_ref, *refs):
        total = refs[0][...].astype(WIDE)
        for k in range(1, 4):
            total = total + refs[k][...].astype(WIDE)
        total = total.astype(LOW)
        part = refs[8]
        part[...] = dot(total[:, :384], refs[4][...], 1, 1) + dot(total[:, 384:], refs[5][...], 1, 1)
        mine = pl.multiple_of(at_ref[0] * 384, 128)
        theirs = pl.multiple_of((1 - at_ref[0]) * 384, 128)
        refs[6][...] = part[:, pl.ds(mine, 384)]
        refs[7][...] = part[:, pl.ds(theirs, 384)].astype(LOW)

    return whole_kernel(
        body,
        [wide_array(64, 384), low_array(64, 384)],
        (tensor_at, *pieces, wk, wv),
        "store_finish",
        1,
        scratch=[pltpu.VMEM((64, 768), WIDE)],
        scalars=1,
    )


def sum_block(grads_ref, got_ref, rows, start, col, width):
    cols = pl.ds(pl.multiple_of(start + col, 128), width)
    return grads_ref[rows, cols].astype(WIDE) + got_ref[rows, col : col + width].astype(WIDE)


def ffn_grads(place, h_two, d_pre, e_three, act, after):
    def body(place_ref, h_ref, d_ref, e_ref, a_ref, mine_ref, theirs_ref):
        first = place_ref[3] == 0
        for left, right, is_mine in ((h_ref, d_ref, first), (e_ref, a_ref, jnp.logical_not(first))):
            for c in range(0, 1536, 512):
                part = dot(left[...], right[:, c : c + 512], 0, 0).astype(LOW)

                @pl.when(is_mine)
                def keep():
                    mine_ref[:, c : c + 512] = part

                @pl.when(jnp.logical_not(is_mine))
                def give():
                    theirs_ref[:, c : c + 512] = part

    return whole_kernel(
        body,
        [low_array(768, 1536)] * 2,
        (place, h_two, d_pre, e_three, act),
        "ffn_grads",
        3,
        scalars=1,
        after=after,
    )


def ring_pieces(place_ref, block_of, outs):
    for k in range(4):
        at_y = ((place_ref[0] - k) & 3) * 192
        at_x = ((place_ref[1] - k) & 3) * 48
        for part in range(4):
            to = slice(part * 48, part * 48 + 48)
            half_to = slice(part % 2 * 48, part % 2 * 48 + 48)
            for g in range(2):
                row = at_y + part * 48 if g == 0 else part * 192 + at_x
                block = block_of(g, pl.ds(pl.multiple_of(row, 16), 48))
                if k == 0:
                    outs[5 * g][to, :] = block
                elif k == 2:
                    outs[5 * g + 3 + part // 2][half_to, :] = block.astype(LOW)
                else:
                    outs[5 * g + (k + 1) // 2][to, :] = block.astype(LOW)


def ring_shapes(widths):
    shapes = []
    for width in widths:
        shapes += [wide_array(192, width)] + [low_array(192, width)] * 2
        shapes += [low_array(96, width)] * 2
    return shapes


def ring_halves(pieces):
    halves = (
        shift(pieces[3], "y", -1),
        shift(pieces[4], "y", 1),
        shift(pieces[8], "x", -1),
        shift(pieces[9], "x", 1),
    )
    sums = ring_middle((pieces[1], pieces[2], pieces[6], pieces[7]), halves)
    return sums, (
        (shift(sums[0], "y", -1), shift(sums[1], "y", 1)),
        (shift(sums[2], "x", -1), shift(sums[3], "x", 1)),
    )


def early_first(place, grads, got):
    width = grads.shape[1] // 2

    def body(place_ref, grads_ref, got_ref, *outs):
        def block_of(g, rows):
            cols = slice(g * width, (g + 1) * width)
            return grads_ref[rows, cols].astype(WIDE) + got_ref[rows, cols].astype(WIDE)

        ring_pieces(place_ref, block_of, outs)

    shapes = ring_shapes((width, width))
    return whole_kernel(body, shapes, (place, grads, got), "early_first", 3, scalars=1)


def ring_middle(sides, got):
    def body(*refs):
        for g in range(2):
            for j in range(2):
                ref, half, out = refs[2 * g + j], refs[4 + 2 * g + j], refs[8 + 2 * g + j]
                summed, kept = (slice(0, 96), slice(96, 192))[:: 1 - 2 * j]
                both = ref[summed, :].astype(WIDE) + half[...].astype(WIDE)
                out[summed, :] = both.astype(LOW)
                out[kept, :] = ref[kept, :]

    return whole_kernel(
        body, [low_array(*side.shape) for side in sides], (*sides, *got), "ring_middle", 1
    )


LATE_ONE, LATE_TWO = 768, 896
LATE_HALF = 1280


def late_first(place, grads, got, store_mine, store_got, after):
    middle = LATE_HALF - LATE_ONE

    def body(place_ref, grads_ref, got_ref, store_ref, store_got_ref, *outs):
        start = place_ref[3] * LATE_HALF

        def block_of(g, rows):
            if g == 0:
                return sum_block(grads_ref, got_ref, rows, start, 0, LATE_ONE)
            block = sum_block(grads_ref, got_ref, rows, start, LATE_ONE, middle)
            store = store_ref[rows, :].astype(WIDE) + store_got_ref[rows, :].astype(WIDE)
            return jnp.concatenate([block, store], axis=1)

        ring_pieces(place_ref, block_of, outs)

    return whole_kernel(
        body,
        ring_shapes((LATE_ONE, LATE_TWO)),
        (place, grads, got, store_mine, store_got),
        "late_first",
        3,
        scalars=1,
        after=after,
    )


def weights_second(place, groups, after):
    ways = [way for way, _, _ in groups]
    counts = [1 + len(got) for _, _, got in groups]
    widths = [own.shape[1] for _, own, _ in groups]
    flat = [a for _, own, got in groups for a in (own, *got)]

    def body(place_ref, *refs):
        ins, outs = refs[: len(flat)], refs[len(flat) :]
        starts = [0, 0]
        first = 0
        for way, count, width in zip(ways, counts, widths):
            cols = slice(starts[way], starts[way] + width)
            starts[way] += width
            for k in range(4):
                at = (place_ref[1 - way] - k) & 3
                rows = pl.ds(pl.multiple_of(at * 48, 16), 48)
                block = ins[first][rows, :]
                for j in range(1, count):
                    block = block + ins[first + j][rows, :].astype(WIDE)
                outs[4 * way + k][:, cols] = block if k == 0 else block.astype(LOW)
            first += count

    out_shape = []
    for way in range(2):
        width = sum(w for w, at in zip(widths, ways) if at == way)
        out_shape += [wide_array(48, width)] + [low_array(48, width)] * 3
    return whole_kernel(
        body, out_shape, (place, *flat), "weights_second", 1, scalars=1, after=after
    )


def pick(pieces, index):
    chosen = pieces[0]
    for k in range(1, len(pieces)):
        chosen = jnp.where(index == k, pieces[k], chosen)
    return chosen


def weights_third(place, own, got):
    widths = [o.shape[1] for o in own]
    groups, total_width = len(own), sum(widths)

    def body(place_ref, *refs):
        ins, outs = refs[: 4 * groups], refs[4 * groups :]
        start = 0
        for g in range(groups):
            total = ins[g][...]
            for k in range(3):
                total = total + ins[groups + 3 * g + k][...].astype(WIDE)
            pieces = [total[k * 12 : (k + 1) * 12, :] for k in range(4)]
            cols = slice(start, start + widths[g])
            start += widths[g]
            for k in range(4):
                block = pick(pieces, (place_ref[2] - k) & 3)
                outs[k][:, cols] = block if k == 0 else block.astype(LOW)

    flat = [piece for three in got for piece in three]
    return whole_kernel(
        body,
        [wide_array(12, total_width)] + [low_array(12, total_width)] * 3,
        (place, *own, *flat),
        "weights_third",
        1,
        scalars=1,
    )


def weights_fourth(place, own, got):
    width = own.shape[1]

    def body(place_ref, *refs):
        total = refs[0][...]
        for k in range(3):
            total = total + refs[1 + k][...].astype(WIDE)
        pieces = [total[:6, :], total[6:, :]]
        refs[4][...] = pick(pieces, place_ref[3])
        refs[5][...] = pick(pieces, 1 - place_ref[3]).astype(LOW)

    return whole_kernel(
        body,
        [wide_array(6, width), low_array(6, width)],
        (place, own, *got),
        "weights_fourth",
        1,
        scalars=1,
    )


def to_other_core(grads):
    half = grads.shape[1] // 2
    theirs = lax.dynamic_slice_in_dim(grads, (1 - coord("core")) * half, half, 1)
    return shift(theirs, "core", 1)


def causal_bias(tokens):
    key = lax.broadcasted_iota(jnp.int32, (tokens, tokens), 0)
    query = lax.broadcasted_iota(jnp.int32, (tokens, tokens), 1)
    return jnp.where(key <= query, 0.0, MASKED)


def self_fwd_kernel(
    x_ref, wq_ref, wk_ref, wv_ref, wo_ref, q_ref, k_ref, v_ref, mixt_ref, mix_ref, lse_ref, part_ref
):
    x = x_ref[...]
    tokens = x.shape[0]
    q_ref[...] = dot(x, wq_ref[...]).astype(LOW) * jnp.asarray(SCALE, LOW)
    k_ref[...] = dot(x, wk_ref[...]).astype(LOW)
    v_ref[...] = dot(x, wv_ref[...]).astype(LOW)
    bias = causal_bias(tokens)
    lse_ref[...] = jnp.zeros_like(lse_ref)
    for pair in range(3):
        cols = slice(pair * 128, (pair + 1) * 128)
        queries, keys, values = q_ref[:, cols], k_ref[:, cols], v_ref[:, cols]
        for a in range(2):
            h = 2 * pair + a
            scores = dot(keys, first_half_lanes(queries, a), 1, 1) + bias
            top = jnp.max(scores, axis=0, keepdims=True)
            weights = jnp.exp(scores - top)
            total = jnp.sum(weights, axis=0, keepdims=True)
            mixed = dot(values, weights.astype(LOW), 0, 0)[a * HEAD_DIM : (a + 1) * HEAD_DIM, :]
            mixt_ref[h * HEAD_DIM : (h + 1) * HEAD_DIM, :] = mixed / total
            lse_ref[h : h + 1, :] = top + jnp.log(total)
    mix_ref[...] = mixt_ref[...].T.astype(LOW)
    part_ref[...] = dot(mix_ref[...], wo_ref[...]).astype(LOW)


def self_fwd(x, wq, wk, wv, wo):
    tokens = x.shape[0]
    narrow = low_array(tokens, 384)
    out_shape = [narrow, narrow, narrow, wide_array(384, tokens), narrow, wide_array(8, tokens)]
    out_shape.append(low_array(tokens, 768))
    return whole_kernel(self_fwd_kernel, out_shape, (x, wq, wk, wv, wo), "self_fwd", 3)


def self_bwd_kernel(
    e_ref,
    q_ref,
    k_ref,
    v_ref,
    mixt_ref,
    lse_ref,
    wq_ref,
    wk_ref,
    wv_ref,
    wo_ref,
    dq_ref,
    dk_ref,
    dv_ref,
    part_ref,
    dqt_s,
):
    tokens = e_ref.shape[0]
    dm = dot(e_ref[...], wo_ref[...], 1, 1).astype(LOW)
    dmt = dm.astype(WIDE).T
    bias = causal_bias(tokens)
    for pair in range(3):
        cols = slice(pair * 128, (pair + 1) * 128)
        queries, keys, values, dm_pair = q_ref[:, cols], k_ref[:, cols], v_ref[:, cols], dm[:, cols]
        dk = dv = None
        for a in range(2):
            h = 2 * pair + a
            rows = slice(h * HEAD_DIM, (h + 1) * HEAD_DIM)
            q_head = first_half_lanes(queries, a)
            dm_head = first_half_lanes(dm_pair, a)
            inner = jnp.sum(dmt[rows, :] * mixt_ref[rows, :], axis=0, keepdims=True)
            scores = dot(keys, q_head, 1, 1) + bias
            probs = jnp.exp(scores - lse_ref[h : h + 1, :])
            dp = dot(values, dm_head, 1, 1)
            ds = (probs * (dp - inner)).astype(LOW)
            dv_head = dot(probs.astype(LOW), dm_head)
            dk_head = dot(ds, q_head)
            dk = dk_head if a == 0 else dk + dk_head
            dv = dv_head if a == 0 else dv + dv_head
            dqt_s[rows, :] = dot(keys, ds, 0, 0)[a * HEAD_DIM : (a + 1) * HEAD_DIM, :] * SCALE
        dk_ref[:, cols] = dk.astype(LOW)
        dv_ref[:, cols] = dv.astype(LOW)
    dq_ref[...] = dqt_s[...].T.astype(LOW)
    part_ref[...] = (
        dot(dq_ref[...], wq_ref[...], 1, 1)
        + dot(dk_ref[...], wk_ref[...], 1, 1)
        + dot(dv_ref[...], wv_ref[...], 1, 1)
    ).astype(LOW)


def self_bwd(e_one, q, k, v, mixt, lse, wq, wk, wv, wo, after):
    tokens = e_one.shape[0]
    return whole_kernel(
        self_bwd_kernel,
        [low_array(tokens, 384)] * 3 + [low_array(tokens, 768)],
        (e_one, q, k, v, mixt, lse, wq, wk, wv, wo),
        "self_bwd",
        3,
        scratch=[pltpu.VMEM((384, tokens), WIDE)],
        after=after,
    )


def layer_norm(summed, gain_vec, bias_vec):
    row_mean = jnp.mean(summed, axis=-1, keepdims=True)
    centred = summed - row_mean
    variance = jnp.mean(centred * centred, axis=-1, keepdims=True)
    inv_std = lax.rsqrt(variance + 1e-05)
    normed = centred * inv_std
    return (normed * gain_vec + bias_vec, normed, inv_std)


def norm_back(grad_out, normed, inv_std, gain_vec):
    grad_normed = grad_out * gain_vec
    centre_term = jnp.mean(grad_normed, axis=-1, keepdims=True)
    slope_term = jnp.mean(grad_normed * normed, axis=-1, keepdims=True)
    grad_in = inv_std * (grad_normed - centre_term - normed * slope_term)
    return (grad_in, jnp.sum(grad_out * normed, axis=0), jnp.sum(grad_out, axis=0))


def shards(
    x_in,
    lengths,
    retrieved,
    datastore,
    self_wq,
    self_wk,
    self_wv,
    self_wo,
    ln1_gain,
    ln1_bias,
    cross_wq,
    cross_wk,
    cross_wv,
    cross_wo,
    ln2_gain,
    ln2_bias,
    ffn_w1,
    ffn_w2,
    ln3_gain,
    ln3_bias,
    cotangent,
):
    tokens = x_in.shape[0]
    positions = lax.iota(jnp.int32, tokens)
    place = jnp.stack([coord("y"), coord("x"), coord("z"), coord("core")]).astype(jnp.int32)
    tensor_at = lax.axis_index("tensor").astype(jnp.int32).reshape(1)

    local = project_store(datastore, cross_wk, cross_wv)
    near = [local] + shifts(local, "z")
    q_self, k_self, v_self, mixt_self, mix_self, lse_self, part = self_fwd(
        x_in, self_wq, self_wk, self_wv, self_wo
    )
    mask_one = retrieval_mask(place, retrieved, 0, (part,))
    near_a, near_b = join_near(near, (mask_one,))
    one_a, three_a = neighbours(near_a, "x")
    one_b, three_b = neighbours(near_b, "y")
    low_a, high_a, low_b, high_b = pass_on(halve(one_a, three_a, one_b, three_b, ()), "x", "y")
    kv_a, kv_b, kv_zero, states_a, states_b = join_four(
        (near_a, one_a, three_a, low_a, high_a), (near_b, one_b, three_b, low_b, high_b), ()
    )
    mask_two = retrieval_mask(place, retrieved, 1, (kv_a,))
    bias = (mask_one, mask_two)
    far_zero = shift(kv_zero, "core", 1)
    one_a, three_a = neighbours(kv_a, "y")
    one_b, three_b = neighbours(kv_b, "x")
    cut = halve(one_a, three_a, one_b, three_b, (mask_two,))
    low_a, high_a, low_b, high_b = pass_on(cut, "y", "x")

    h_one, normed_one, inv_one = layer_norm(
        x_in.astype(WIDE) + tensor_total(part), ln1_gain, ln1_bias
    )
    h_one_low = h_one.astype(LOW)
    q_cross = dot(h_one_low, cross_wq).astype(LOW) * jnp.asarray(SCALE, LOW)
    qt_cross = q_cross.T
    one_block = (((0, 0, 1024, 0),),)
    two_blocks = (((0, 0, 1024, 0),), ((0, 1024, 1024, 0),))
    state = cross_fwd(qt_cross, bias, (0,), one_block, (kv_zero,), after=(cut[0],))
    *state, kv_sides = cross_fwd(
        qt_cross,
        bias,
        (1, 3),
        (((0, 0, 512, 0), (1, 0, 512, 512)), ((2, 0, 512, 0), (3, 0, 512, 512))),
        (one_a, one_b, three_a, three_b),
        state,
        collect=True,
        after=(far_zero,),
    )
    far_sides = shift(kv_sides, "core", 1)
    *state, kv_two = cross_fwd(
        qt_cross,
        bias,
        (2,),
        (((0, 0, 256, 0), (1, 0, 256, 256), (2, 0, 256, 512), (3, 0, 256, 768)),),
        (low_a, high_a, low_b, high_b),
        state,
        collect=True,
    )
    far_two = shift(kv_two, "core", 1)
    state = cross_fwd(
        qt_cross,
        bias,
        (4, 5, 7),
        (((1, 0, 1024, 0),),) + two_blocks,
        (far_sides, far_zero),
        state,
    )
    mixt_cross, mix_cross, lse_cross = cross_fwd(
        qt_cross, bias, (6,), one_block, (far_two,), state, last=True
    )
    h_two, normed_two, inv_two = layer_norm(
        h_one + tensor_total(dot(mix_cross, cross_wo)), ln2_gain, ln2_bias
    )
    h_two_low = h_two.astype(LOW)
    pre_act = dot(h_two_low, ffn_w1)
    act_low = jax.nn.gelu(pre_act).astype(LOW)
    h_three, normed_three, inv_three = layer_norm(
        h_two + tensor_total(dot(act_low, ffn_w2)), ln3_gain, ln3_bias
    )
    row_valid = (positions < lengths[0]).astype(WIDE)[:, None]
    block_out = (h_three * row_valid).astype(LOW)

    grad_out = cotangent.astype(WIDE) * row_valid
    d_three, grad_g3, grad_b3 = norm_back(grad_out, normed_three, inv_three, ln3_gain)
    e_three = d_three.astype(LOW)
    d_act = dot(e_three, ffn_w2, 1, 1)
    unused, gelu_back = jax.vjp(jax.nn.gelu, pre_act)
    d_pre = gelu_back(d_act)[0].astype(LOW)
    ffn_part = dot(d_pre, ffn_w1, 1, 1).astype(LOW)
    d_h_two = d_three + (ffn_part.astype(WIDE) + other_tensor(ffn_part).astype(WIDE))
    early_mine, early_theirs = ffn_grads(place, h_two_low, d_pre, e_three, act_low, (ffn_part,))
    early_got = shift(early_theirs, "core", 1)

    d_two, grad_g2, grad_b2 = norm_back(d_h_two, normed_two, inv_two, ln2_gain)
    e_two = d_two.astype(LOW)
    dm_cross = dot(e_two, cross_wo, 1, 1).astype(LOW)
    dmt_cross = dm_cross.T
    inner = jnp.sum((dmt_cross.astype(WIDE) * mixt_cross).reshape(6, HEAD_DIM, tokens), axis=1)
    inner = jnp.concatenate([inner, jnp.zeros((2, tokens), WIDE)], axis=0)
    early = early_first(place, early_mine, early_got)
    near_sums, early_yx = ring_halves(early)
    sides = (qt_cross, q_cross, dmt_cross, dm_cross, lse_cross, inner)

    dqt, far = cross_bwd(
        sides,
        jnp.zeros((384, tokens), WIDE),
        bias,
        (6, 5),
        (((0, 0, 1024, 0),), ((1, 0, 1024, 0),)),
        (far_two, far_sides),
        ((0, 0, 2048),),
        after=(near_sums[0],),
    )
    got_two_one = shift(far, "core", 1)
    dqt, far = cross_bwd(
        sides,
        dqt,
        bias,
        (7, 4),
        (((0, 1024, 1024, 0),), ((1, 0, 1024, 0),)),
        (far_sides, far_zero),
        ((0, 0, 2048),),
        after=(*early_yx[0], *early_yx[1]),
    )
    got_three_zero = shift(far, "core", 1)
    dqt, low_a, high_a, low_b, high_b = cross_bwd(
        sides,
        dqt,
        bias,
        (2,),
        one_block,
        (kv_two,),
        tuple((0, k * 256, 256) for k in range(4)),
        adds=one_block,
        add_arrays=(got_two_one,),
    )
    low_a, low_b = shift(low_a, "y", -1), shift(low_b, "x", -1)
    high_a, high_b = shift(high_a, "y", 1), shift(high_b, "x", 1)
    dqt, own_a, own_b = cross_bwd(
        sides,
        dqt,
        bias,
        (0,),
        one_block,
        (kv_zero,),
        ((0, 0, 512), (0, 512, 512)),
        adds=(((0, 1024, 1024, 0),),),
        add_arrays=(got_three_zero,),
    )
    dqt, one_a, one_b, three_a, three_b = cross_bwd(
        sides,
        dqt,
        bias,
        (1, 3),
        two_blocks,
        (kv_sides,),
        ((0, 0, 512), (0, 512, 512), (1, 0, 512), (1, 512, 512)),
        adds=(((0, 1024, 1024, 0),), ((1, 0, 1024, 0),)),
        add_arrays=(got_two_one, got_three_zero),
        halves=(((0, 0, 256, 0), (1, 0, 256, 256)), ((2, 0, 256, 0), (3, 0, 256, 256))),
        half_arrays=(low_a, low_b, high_a, high_b),
    )
    got_a = [shift(one_a, "y", -1), shift(three_a, "y", 1)]
    got_b = [shift(one_b, "x", -1), shift(three_b, "x", 1)]

    blocks = store_sum_far((own_a, own_b), (got_a, got_b))
    got_a, got_b = returns(blocks[1:4], "x"), returns(blocks[5:8], "y")

    dqt_low = (dqt * SCALE).astype(LOW)
    d_h_one = d_two + tensor_total(dot(dqt_low, cross_wq, 0, 1))
    d_one, grad_g1, grad_b1 = norm_back(d_h_one, normed_one, inv_one, ln1_gain)
    e_one = d_one.astype(LOW)
    dq_self, dk_self, dv_self, part = self_bwd(
        e_one,
        q_self,
        k_self,
        v_self,
        mixt_self,
        lse_self,
        self_wq,
        self_wk,
        self_wv,
        self_wo,
        (blocks[1],),
    )
    part_got = other_tensor(part)
    input_grad = d_one + (part.astype(WIDE) + part_got.astype(WIDE))
    vectors = jnp.stack([grad_g1, grad_b1, grad_g2, grad_b2, grad_g3, grad_b3], axis=1)
    grads = [
        dot(x_in, dq_self, 0, 0),
        dot(x_in, dk_self, 0, 0),
        dot(x_in, dv_self, 0, 0),
        dot(e_one, mix_self, 0, 0),
        dot(h_one_low, dqt_low, 0, 1),
        dot(e_two, mix_cross, 0, 0),
        jnp.pad(vectors, ((0, 0), (0, 250))),
    ]
    grads = jnp.concatenate([g.astype(LOW) for g in grads], axis=1)
    late_got = to_other_core(grads)

    store_keep, store_give = store_weight_grads(place, (states_a, states_b), blocks)
    pieces = store_sum_mid((blocks[0], blocks[4]), (got_a, got_b))
    late = late_first(
        place, grads, late_got, store_keep, shift(store_give, "core", 1), (pieces[1], part_got)
    )
    late_sums, late_yx = ring_halves(late)
    pieces = [pieces[0]] + returns(pieces[1:], "z")
    store_mine, store_send = store_finish(tensor_at, pieces, cross_wk, cross_wv)
    datastore_grad = store_mine + other_tensor(store_send).astype(WIDE)

    groups = (
        (0, late[0], late_yx[0]),
        (0, early[0], early_yx[0]),
        (1, late[5], late_yx[1]),
        (1, early[5], early_yx[1]),
    )
    blocks = weights_second(place, groups, (store_send,))
    late_xy = (returns(blocks[1:4], "x"), returns(blocks[5:8], "y"))
    last = weights_third(place, (blocks[0], blocks[4]), late_xy)
    keep, send = weights_fourth(place, last[0], returns(last[1:], "z"))
    got = shift(send, "core", 1).astype(WIDE)
    first = coord("core") == 0
    parts = (jnp.where(first, keep, got), jnp.where(first, got, keep))
    late_sum = jnp.concatenate(
        [c for h in parts for c in (h[:, :768], h[:, 1536:2048])], axis=1
    )
    store_sum = jnp.concatenate([h[:, 2048:2432] for h in parts], axis=1)
    grad_w1, grad_w2 = [jnp.concatenate([h[:, 768:1536], h[:, 2432:]], axis=1) for h in parts]

    part_of = lambda k: late_sum[:, k * 384 : (k + 1) * 384]
    vector = lambda k: late_sum[:, 2304 + k]
    return (
        block_out,
        input_grad,
        datastore_grad,
        part_of(0),
        part_of(1),
        part_of(2),
        part_of(3).T,
        vector(0),
        vector(1),
        part_of(4),
        store_sum[:, :384],
        store_sum[:, 384:],
        part_of(5).T,
        vector(2),
        vector(3),
        grad_w1,
        grad_w2.T,
        vector(4),
        vector(5),
    )


def solution(mesh):
    rows, columns, split = P("dp", None), P(None, "tensor"), P("tensor", None)
    norm = (P(), P())
    in_specs = (
        (rows, P("dp"), rows, rows)
        + (columns, columns, columns, split)
        + norm
        + (columns, columns, columns, split)
        + norm
        + (columns, split)
        + norm
        + (rows,)
    )
    both, turned, vector = P("dp", "tensor"), P("tensor", "dp"), P("dp")
    out_specs = (
        (rows, rows, both)
        + (both, both, both, turned)
        + (vector, vector)
        + (both, both, both, turned)
        + (vector, vector)
        + (both, turned)
        + (vector, vector)
    )
    return jax.shard_map(shards, mesh=mesh, in_specs=in_specs, out_specs=out_specs, check_vma=False)
```

```python
import functools

import jax
import jax.numpy as jnp
from jax import lax
from jax.experimental import pallas as pl
from jax.experimental.pallas import tpu as pltpu
from jax.sharding import PartitionSpec as P

LOW = jnp.bfloat16
WIDE = jnp.float32
MASKED = -1e30
HEAD_DIM = 64
SCALE = 0.125
AXES = {"y": (4, 32), "x": (4, 8), "z": (4, 2), "core": (2, 1)}
N_DP = 128
VMEM = 26 * 2**20


def dot(left, right, left_dim=1, right_dim=0):
    return lax.dot_general(
        left, right, (((left_dim,), (right_dim,)), ((), ())), preferred_element_type=WIDE
    )


def coord(axis):
    size, stride = AXES[axis]
    return (lax.axis_index("dp") // stride) % size


def shift(value, axis, step):
    size, stride = AXES[axis]
    pairs = []
    for d in range(N_DP):
        at = (d // stride) % size
        pairs.append((d, d + ((at + step) % size - at) * stride))
    return lax.ppermute(value, "dp", pairs)


def other_tensor(value):
    return lax.ppermute(value, "tensor", [(0, 1), (1, 0)])


def tensor_total(partial_value):
    mine = partial_value.astype(LOW)
    return mine.astype(WIDE) + other_tensor(mine).astype(WIDE)


def shifts(value, axis):
    return [shift(value, axis, k) for k in range(1, AXES[axis][0])]


def returns(pieces, axis):
    return [shift(piece, axis, -1 - k) for k, piece in enumerate(pieces)]


def neighbours(block, axis):
    one, three = shift(block, axis, 1), shift(block, axis, -1)
    return one, three


def whole_kernel(body, out_shape, args, name, microseconds, scratch=(), scalars=0, after=()):
    spec = lambda a: pl.BlockSpec(a.shape, lambda i: (0,) * len(a.shape))
    in_specs = [pl.BlockSpec(memory_space=pltpu.SMEM)] * scalars
    in_specs += [spec(a) for a in args[scalars:]]
    in_specs += [pl.BlockSpec(memory_space=pl.ANY)] * len(after)
    out_specs = [spec(a) for a in out_shape] if isinstance(out_shape, list) else spec(out_shape)
    used, skipped = len(args), len(args) + len(after)

    def kernel(*refs):
        body(*refs[:used], *refs[skipped:])

    return pl.pallas_call(
        kernel,
        out_shape=out_shape,
        grid=(1,),
        in_specs=in_specs,
        out_specs=out_specs,
        scratch_shapes=list(scratch),
        compiler_params=pltpu.CompilerParams(vmem_limit_bytes=VMEM),
        cost_estimate=cost(microseconds, 1e6),
        name=name,
    )(*args, *after)


def cost(microseconds, moved):
    return pl.CostEstimate(
        flops=int(microseconds * 5e9), bytes_accessed=int(moved), transcendentals=0
    )


def low_array(*shape):
    return jax.ShapeDtypeStruct(shape, LOW)


def wide_array(*shape):
    return jax.ShapeDtypeStruct(shape, WIDE)


def first_half_rows(pair, which):
    row = lax.broadcasted_iota(jnp.int32, pair.shape, 0)
    return jnp.where((row < HEAD_DIM) == (which == 0), pair, jnp.zeros_like(pair))


def first_half_lanes(pair, which):
    lane = lax.broadcasted_iota(jnp.int32, pair.shape, 1)
    return jnp.where((lane < HEAD_DIM) == (which == 0), pair, jnp.zeros_like(pair))


def project_store(datastore, wk, wv):
    def body(s_ref, k_ref, v_ref, out_ref):
        out_ref[:, :384] = dot(s_ref[...], k_ref[...]).astype(LOW)
        out_ref[:, 384:768] = dot(s_ref[...], v_ref[...]).astype(LOW)
        out_ref[:, 768:] = s_ref[...]

    return whole_kernel(body, low_array(64, 1536), (datastore, wk, wv), "project_store", 1)


def join_near(pieces, after):
    def body(*refs):
        for k in range(4):
            refs[4][k * 32 : (k + 1) * 32, :] = refs[k][:32, :]
            refs[5][k * 32 : (k + 1) * 32, :] = refs[k][32:, :]

    return whole_kernel(body, [low_array(128, 1536)] * 2, pieces, "join_near", 1, after=after)


def halve(one_a, three_a, one_b, three_b, after):
    rows, width = one_a.shape
    half = rows // 2

    def body(*refs):
        for k in range(4):
            refs[4 + k][...] = refs[k][:half, :] if k % 2 == 0 else refs[k][half:, :]

    return whole_kernel(
        body, [low_array(half, width)] * 4, (one_a, three_a, one_b, three_b), "halve", 1, after=after
    )


def pass_on(halves, axis_a, axis_b):
    low_a, high_a, low_b, high_b = halves
    return (
        shift(low_a, axis_a, 1),
        shift(high_a, axis_a, -1),
        shift(low_b, axis_b, 1),
        shift(high_b, axis_b, -1),
    )


def join_four(pieces_a, pieces_b, after):
    def body(*refs):
        ins, outs = refs[:10], refs[10:]
        for g in range(2):
            own, one, three, low, high = ins[5 * g : 5 * g + 5]
            for ref, at in ((own, 0), (one, 128), (low, 256), (high, 320), (three, 384)):
                rows = slice(at, at + ref.shape[0])
                outs[g][rows, :] = ref[:, :768]
                outs[2][g * 512 + at : g * 512 + at + ref.shape[0], :] = ref[:, :768]
                outs[3 + g][rows, :] = ref[:, 768:]

    out_shape = [low_array(512, 768)] * 2 + [low_array(1024, 768)] + [low_array(512, 768)] * 2
    return whole_kernel(body, out_shape, (*pieces_a, *pieces_b), "join_four", 2, after=after)


def mask_body(place_ref, picks_ref, out_ref, high_s, low_s, count_s):
    picks = picks_ref[...]
    core = (place_ref[3] - (picks >> 6)) & 1
    at_z = (place_ref[2] - (picks >> 7)) & 3
    at_x = (place_ref[1] - (picks >> 9)) & 3
    at_y = (place_ref[0] - (picks >> 11)) & 3
    group = (picks >> 5) & 1
    chunk = jnp.where(group == 0, at_y, at_x)
    inside = jnp.where(group == 0, at_x, at_y)
    high_s[...] = (core << 5) | (chunk << 3) | (group << 2) | inside
    low_s[...] = (at_z << 5) | (picks & 31)
    rows, k_top = picks_ref.shape

    def count(t, carry):
        high = high_s[pl.ds(t, 1), :]
        low = low_s[pl.ds(t, 1), :]
        is_high = lax.broadcasted_iota(jnp.int32, (64, k_top), 0) == high
        is_low = lax.broadcasted_iota(jnp.int32, (128, k_top), 0) == low
        count_s[pl.ds(pl.multiple_of(t * 64, 64), 64), :] = dot(
            jnp.where(is_high, 1.0, 0.0).astype(jnp.float8_e4m3fn),
            jnp.where(is_low, 1.0, 0.0).astype(jnp.float8_e4m3fn),
            1,
            1,
        )
        return carry

    lax.fori_loop(0, rows, count, 0, unroll=8)

    def turn(h, carry):
        block = count_s[pl.ds(h, rows, stride=64), :]
        bias = jnp.where(block.T > 0.5, 0.0, MASKED)
        out_ref[pl.ds(pl.multiple_of(h * 128, 128), 128), :] = bias.astype(LOW)
        return carry

    lax.fori_loop(0, 64, turn, 0, unroll=2)


def retrieval_mask(place, picks, part, after):
    tokens, k_top = picks.shape
    rows = tokens // 2

    def kernel(place_ref, picks_ref, *refs):
        mask_body(place_ref, picks_ref, *refs[len(after) :])

    return pl.pallas_call(
        kernel,
        out_shape=low_array(8192, rows),
        grid=(1,),
        in_specs=[
            pl.BlockSpec(memory_space=pltpu.SMEM),
            pl.BlockSpec((rows, k_top), lambda i: (part, 0)),
        ]
        + anywhere(len(after)),
        out_specs=pl.BlockSpec((8192, rows), lambda i: (0, 0)),
        scratch_shapes=[
            pltpu.VMEM((rows, k_top), jnp.int32),
            pltpu.VMEM((rows, k_top), jnp.int32),
            pltpu.VMEM((rows * 64, 128), WIDE),
        ],
        compiler_params=pltpu.CompilerParams(vmem_limit_bytes=VMEM),
        cost_estimate=cost(17, 3e6),
        name="retrieval_mask",
    )(place, picks, *after)


def load_blocks(blocks, refs, into, sems, column):
    for i, pieces in enumerate(blocks):
        for operand, row, rows, to in pieces:
            pltpu.make_async_copy(
                refs[operand].at[pl.ds(row, rows)],
                into.at[i, pl.ds(to, rows)],
                sems.at[i, column],
            ).start()

    def wait(i):
        pltpu.make_async_copy(into.at[i], into.at[i], sems.at[i, column]).wait()

    return wait


def load_masks(chunks, bias_refs, into, sems, column):
    for i, chunk in enumerate(chunks):
        for j in range(2):
            pltpu.make_async_copy(
                bias_refs[j].at[pl.ds(chunk * 1024, 1024)],
                into.at[i, :, pl.ds(j * 128, 128)],
                sems.at[i, column],
            ).start()

    def wait(i):
        pltpu.make_async_copy(into.at[i], into.at[i], sems.at[i, column]).wait()

    return wait


def in_vmem(count):
    return [pl.BlockSpec(memory_space=pltpu.VMEM)] * count


def anywhere(count):
    return [pl.BlockSpec(memory_space=pl.ANY)] * count


def cross_fwd_body(chunks, blocks, counts, first, last, collect, *refs):
    n = len(chunks)
    n_arrays, n_after = counts
    qt_ref, refs = refs[0], refs[1:]
    if not first:
        state, refs = refs[:3], refs[3:]
    bias_refs, arrays, refs = refs[:2], refs[2 : 2 + n_arrays], refs[2 + n_arrays + n_after :]
    outs, refs = refs[:3], refs[3:]
    if collect:
        collected, refs = refs[0], refs[1:]
    kv_s, bias_s, sems, out_sem = refs[:4]
    if last:
        mixt_ref, mix_ref, lse_ref = outs
        acc, top_s, sum_s = refs[4:]
    else:
        acc, top_s, sum_s = outs
    wait_kv = load_blocks(blocks, arrays, kv_s, sems, 0)
    wait_bias = load_masks(chunks, bias_refs, bias_s, sems, 1)
    if first:
        acc[...] = jnp.zeros_like(acc)
        top_s[...] = jnp.full_like(top_s, MASKED)
        sum_s[...] = jnp.zeros_like(sum_s)
    else:
        acc[...] = state[0][...]
        top_s[...] = state[1][...]
        sum_s[...] = state[2][...]

    def step(i, carry):
        wait_kv(i)
        if collect:
            rows = pl.ds(pl.multiple_of(i * 1024, 1024), 1024)
            pltpu.make_async_copy(kv_s.at[i], collected.at[rows], out_sem).start()
        wait_bias(i)
        bias = bias_s[i].astype(WIDE)
        for pair in range(3):
            cols = slice(pair * 128, (pair + 1) * 128)
            keys = kv_s[i, :, cols]
            values = kv_s[i, :, 384 + pair * 128 : 512 + pair * 128]
            queries = qt_ref[cols, :]
            for a in range(2):
                h = 2 * pair + a
                rows = slice(h * HEAD_DIM, (h + 1) * HEAD_DIM)
                scores = dot(keys, first_half_rows(queries, a)) + bias
                old = top_s[h : h + 1, :]
                top = jnp.maximum(old, jnp.max(scores, axis=0, keepdims=True))
                fade = jnp.exp(old - top)
                weights = jnp.exp(scores - top)
                sum_s[h : h + 1, :] = sum_s[h : h + 1, :] * fade + jnp.sum(
                    weights, axis=0, keepdims=True
                )
                top_s[h : h + 1, :] = top
                mixed = dot(values, weights.astype(LOW), 0, 0)
                acc[rows, :] = acc[rows, :] * fade + mixed[a * HEAD_DIM : (a + 1) * HEAD_DIM, :]
        return carry

    lax.fori_loop(0, n, step, 0)
    if last:
        for h in range(6):
            rows = slice(h * HEAD_DIM, (h + 1) * HEAD_DIM)
            acc[rows, :] = acc[rows, :] / sum_s[h : h + 1, :]
        mixt_ref[...] = acc[...]
        mix_ref[...] = acc[...].T.astype(LOW)
        lse_ref[...] = top_s[...] + jnp.log(jnp.maximum(sum_s[...], 1e-30))
    if collect:
        pltpu.make_async_copy(collected, collected, out_sem).wait()


def cross_fwd(
    qt, bias, chunks, blocks, arrays, state=None, last=False, collect=False, after=()
):
    tokens, n = qt.shape[1], len(chunks)
    kept = [wide_array(384, tokens), wide_array(8, tokens), wide_array(8, tokens)]
    scratch = [
        pltpu.VMEM((n, 1024, 768), LOW),
        pltpu.VMEM((n, 1024, tokens), LOW),
        pltpu.SemaphoreType.DMA((n, 2)),
        pltpu.SemaphoreType.DMA,
    ]
    if last:
        out_shape = [kept[0], low_array(tokens, 384), kept[1]]
        scratch += [pltpu.VMEM(a.shape, WIDE) for a in kept]
    else:
        out_shape = list(kept)
    out_specs = in_vmem(3)
    if collect:
        out_shape.append(low_array(n * 1024, 768))
        out_specs += anywhere(1)
    given = (qt,) + (() if state is None else tuple(state))
    return pl.pallas_call(
        functools.partial(
            cross_fwd_body,
            chunks,
            blocks,
            (len(arrays), len(after)),
            state is None,
            last,
            collect,
        ),
        out_shape=out_shape,
        in_specs=in_vmem(len(given)) + anywhere(2 + len(arrays) + len(after)),
        out_specs=out_specs,
        scratch_shapes=scratch,
        compiler_params=pltpu.CompilerParams(vmem_limit_bytes=VMEM),
        cost_estimate=cost(4 * n, 2e6 * n),
        name="cross_fwd",
    )(*given, *bias, *arrays, *after)


def cross_bwd_body(chunks, blocks, adds, halves, pieces, counts, *refs):
    n = len(chunks)
    n_arrays, n_adds, n_halves, n_after = counts
    qt_ref, q_ref, dmt_ref, dm_ref, lse_ref, inner_ref, dq_in = refs[:7]
    bias_refs, refs = refs[7:9], refs[9:]
    arrays, refs = refs[:n_arrays], refs[n_arrays:]
    add_refs, refs = refs[:n_adds], refs[n_adds:]
    half_refs, refs = refs[:n_halves], refs[n_halves + n_after :]
    dq_ref, outs, refs = refs[0], refs[1 : 1 + len(pieces)], refs[1 + len(pieces) :]
    kv_s, bias_s, out_s, sems, out_sems, refs = *refs[:5], refs[5:]
    wait_kv = load_blocks(blocks, arrays, kv_s, sems, 0)
    wait_bias = load_masks(chunks, bias_refs, bias_s, sems, 1)
    if adds:
        add_s = refs[0]
        wait_add = load_blocks(adds, add_refs, add_s, sems, 2)
    if halves:
        half_s = refs[1]
        wait_half = load_blocks(halves, half_refs, half_s, sems, 3)
        for i in range(n):
            wait_add(i)
            wait_half(i)
            for g in range(2):
                at = slice(g * 512 + i * 256, g * 512 + i * 256 + 256)
                both = add_s[i, at, :].astype(WIDE) + half_s[i, g * 256 : g * 256 + 256, :].astype(
                    WIDE
                )
                add_s[i, at, :] = both.astype(LOW)
    dq_ref[...] = dq_in[...]

    def step(i, carry):
        wait_kv(i)
        wait_bias(i)
        if adds and not halves:
            wait_add(i)
        bias = bias_s[i].astype(WIDE)
        for pair in range(3):
            cols = slice(pair * 128, (pair + 1) * 128)
            v_cols = slice(384 + pair * 128, 512 + pair * 128)
            keys, values = kv_s[i, :, cols], kv_s[i, :, v_cols]
            dk = dv = None
            for a in range(2):
                h = 2 * pair + a
                rows = slice(h * HEAD_DIM, (h + 1) * HEAD_DIM)
                scores = dot(keys, first_half_rows(qt_ref[cols, :], a)) + bias
                probs = jnp.exp(scores - lse_ref[h : h + 1, :])
                dp = dot(values, first_half_rows(dmt_ref[cols, :], a))
                ds = (probs * (dp - inner_ref[h : h + 1, :])).astype(LOW)
                dv_head = dot(probs.astype(LOW), first_half_lanes(dm_ref[:, cols], a))
                dk_head = dot(ds, first_half_lanes(q_ref[:, cols], a))
                dk = dk_head if a == 0 else dk + dk_head
                dv = dv_head if a == 0 else dv + dv_head
                dq = dot(keys, ds, 0, 0)
                dq_ref[rows, :] += dq[a * HEAD_DIM : (a + 1) * HEAD_DIM, :]
            if adds:
                dk = dk + add_s[i, :, cols].astype(WIDE)
                dv = dv + add_s[i, :, v_cols].astype(WIDE)
            out_s[i, :, cols] = dk.astype(LOW)
            out_s[i, :, v_cols] = dv.astype(LOW)
        return carry

    if n == 1:
        step(0, 0)
    else:
        lax.fori_loop(0, n, step, 0)
    copies = []
    for j, (i, row, rows) in enumerate(pieces):
        if rows > 1024:
            for b in range(n):
                copies.append(
                    pltpu.make_async_copy(
                        out_s.at[b], outs[j].at[pl.ds(b * 1024, 1024)], out_sems.at[b]
                    )
                )
        else:
            copies.append(
                pltpu.make_async_copy(out_s.at[i, pl.ds(row, rows)], outs[j], out_sems.at[j])
            )
    for copy in copies:
        copy.start()
    for copy in copies:
        copy.wait()


def cross_bwd(
    sides, dq, bias, chunks, blocks, arrays, pieces, adds=(), add_arrays=(), halves=(),
    half_arrays=(), after=(),
):
    tokens, n = dq.shape[1], len(chunks)
    scratch = [
        pltpu.VMEM((n, 1024, 768), LOW),
        pltpu.VMEM((n, 1024, tokens), LOW),
        pltpu.VMEM((n, 1024, 768), LOW),
        pltpu.SemaphoreType.DMA((n, 4)),
        pltpu.SemaphoreType.DMA((max(n, len(pieces)),)),
    ]
    if adds:
        scratch.append(pltpu.VMEM((n, 1024, 768), LOW))
    if halves:
        scratch.append(pltpu.VMEM((n, 512, 768), LOW))
    counts = (len(arrays), len(add_arrays), len(half_arrays), len(after))
    return pl.pallas_call(
        functools.partial(cross_bwd_body, chunks, blocks, adds, halves, pieces, counts),
        out_shape=[wide_array(384, tokens)] + [low_array(rows, 768) for _, _, rows in pieces],
        in_specs=in_vmem(7) + anywhere(2 + sum(counts)),
        out_specs=in_vmem(1) + anywhere(len(pieces)),
        scratch_shapes=scratch,
        compiler_params=pltpu.CompilerParams(vmem_limit_bytes=VMEM),
        cost_estimate=cost(4.5 * n, 4e6 * n),
        name="cross_bwd",
    )(*sides, dq, *bias, *arrays, *add_arrays, *half_arrays, *after)


def store_sum_far(own, got):
    def body(*refs):
        ins, outs = refs[:6], refs[6:]
        for g in range(2):
            total = ins[g][...].astype(WIDE)
            for k in range(2):
                total = total + ins[2 + 2 * g + k][...].astype(WIDE)
            for k in range(4):
                outs[4 * g + k][...] = total[k * 128 : (k + 1) * 128, :].astype(LOW)

    return whole_kernel(
        body, [low_array(128, 768)] * 8, (*own, *got[0], *got[1]), "store_sum_far", 2
    )


def store_weight_grads(place, states, blocks):
    def body(place_ref, *refs):
        sum_s = refs[12]
        for c in range(0, 768, 256):
            total = None
            for g in range(2):
                for k in range(4):
                    part = dot(
                        refs[g][k * 128 : (k + 1) * 128, c : c + 256], refs[2 + 4 * g + k][...], 0, 0
                    )
                    total = part if total is None else total + part
            sum_s[c : c + 256, :] = total.astype(LOW)
        mine = pl.multiple_of(place_ref[3] * 384, 128)
        theirs = pl.multiple_of((1 - place_ref[3]) * 384, 128)
        refs[10][...] = sum_s[:, pl.ds(mine, 384)]
        refs[11][...] = sum_s[:, pl.ds(theirs, 384)]

    return whole_kernel(
        body,
        [low_array(768, 384)] * 2,
        (place, *states, *blocks),
        "store_weight_grads",
        3,
        scratch=[pltpu.VMEM((768, 768), LOW)],
        scalars=1,
    )


def store_sum_mid(own, got):
    def body(*refs):
        ins, outs = refs[:8], refs[8:]
        for g in range(2):
            total = ins[g][...].astype(WIDE)
            for k in range(3):
                total = total + ins[2 + 3 * g + k][...].astype(WIDE)
            for k in range(4):
                outs[k][g * 32 : (g + 1) * 32, :] = total[k * 32 : (k + 1) * 32, :].astype(LOW)

    return whole_kernel(body, [low_array(64, 768)] * 4, (*own, *got[0], *got[1]), "store_sum_mid", 1)


def store_finish(tensor_at, pieces, wk, wv):
    def body(at_ref, *refs):
        total = refs[0][...].astype(WIDE)
        for k in range(1, 4):
            total = total + refs[k][...].astype(WIDE)
        total = total.astype(LOW)
        part = refs[8]
        part[...] = dot(total[:, :384], refs[4][...], 1, 1) + dot(total[:, 384:], refs[5][...], 1, 1)
        mine = pl.multiple_of(at_ref[0] * 384, 128)
        theirs = pl.multiple_of((1 - at_ref[0]) * 384, 128)
        refs[6][...] = part[:, pl.ds(mine, 384)]
        refs[7][...] = part[:, pl.ds(theirs, 384)].astype(LOW)

    return whole_kernel(
        body,
        [wide_array(64, 384), low_array(64, 384)],
        (tensor_at, *pieces, wk, wv),
        "store_finish",
        1,
        scratch=[pltpu.VMEM((64, 768), WIDE)],
        scalars=1,
    )


def sum_block(grads_ref, got_ref, rows, start, col, width):
    cols = pl.ds(pl.multiple_of(start + col, 128), width)
    return grads_ref[rows, cols].astype(WIDE) + got_ref[rows, col : col + width].astype(WIDE)


def ffn_grads(place, h_two, d_pre, e_three, act, after):
    def body(place_ref, h_ref, d_ref, e_ref, a_ref, mine_ref, theirs_ref):
        first = place_ref[3] == 0
        for left, right, is_mine in ((h_ref, d_ref, first), (e_ref, a_ref, jnp.logical_not(first))):
            for c in range(0, 1536, 512):
                part = dot(left[...], right[:, c : c + 512], 0, 0).astype(LOW)

                @pl.when(is_mine)
                def keep():
                    mine_ref[:, c : c + 512] = part

                @pl.when(jnp.logical_not(is_mine))
                def give():
                    theirs_ref[:, c : c + 512] = part

    return whole_kernel(
        body,
        [low_array(768, 1536)] * 2,
        (place, h_two, d_pre, e_three, act),
        "ffn_grads",
        3,
        scalars=1,
        after=after,
    )


def ring_pieces(place_ref, block_of, outs):
    for k in range(4):
        at_y = ((place_ref[0] - k) & 3) * 192
        at_x = ((place_ref[1] - k) & 3) * 48
        for part in range(4):
            to = slice(part * 48, part * 48 + 48)
            half_to = slice(part % 2 * 48, part % 2 * 48 + 48)
            for g in range(2):
                row = at_y + part * 48 if g == 0 else part * 192 + at_x
                block = block_of(g, pl.ds(pl.multiple_of(row, 16), 48))
                if k == 0:
                    outs[5 * g][to, :] = block
                elif k == 2:
                    outs[5 * g + 3 + part // 2][half_to, :] = block.astype(LOW)
                else:
                    outs[5 * g + (k + 1) // 2][to, :] = block.astype(LOW)


def ring_shapes(widths):
    shapes = []
    for width in widths:
        shapes += [wide_array(192, width)] + [low_array(192, width)] * 2
        shapes += [low_array(96, width)] * 2
    return shapes


def ring_halves(pieces, after=()):
    halves = (
        shift(pieces[3], "y", -1),
        shift(pieces[4], "y", 1),
        shift(pieces[8], "x", -1),
        shift(pieces[9], "x", 1),
    )
    sums = ring_middle((pieces[1], pieces[2], pieces[6], pieces[7]), halves, after)
    return sums, (
        (shift(sums[0], "y", -1), shift(sums[1], "y", 1)),
        (shift(sums[2], "x", -1), shift(sums[3], "x", 1)),
    )


def early_first(place, grads, got):
    width = grads.shape[1] // 2

    def body(place_ref, grads_ref, got_ref, *outs):
        def block_of(g, rows):
            cols = slice(g * width, (g + 1) * width)
            return grads_ref[rows, cols].astype(WIDE) + got_ref[rows, cols].astype(WIDE)

        ring_pieces(place_ref, block_of, outs)

    shapes = ring_shapes((width, width))
    return whole_kernel(body, shapes, (place, grads, got), "early_first", 3, scalars=1)


def ring_middle(sides, got, after):
    def body(*refs):
        for g in range(2):
            for j in range(2):
                ref, half, out = refs[2 * g + j], refs[4 + 2 * g + j], refs[8 + 2 * g + j]
                summed, kept = (slice(0, 96), slice(96, 192))[:: 1 - 2 * j]
                both = ref[summed, :].astype(WIDE) + half[...].astype(WIDE)
                out[summed, :] = both.astype(LOW)
                out[kept, :] = ref[kept, :]

    return whole_kernel(
        body,
        [low_array(*side.shape) for side in sides],
        (*sides, *got),
        "ring_middle",
        1,
        after=after,
    )


LATE_ONE, LATE_TWO = 768, 896
LATE_HALF = 1280


def late_first(place, grads, got, store_mine, store_got, after):
    middle = LATE_HALF - LATE_ONE

    def body(place_ref, grads_ref, got_ref, store_ref, store_got_ref, *outs):
        start = place_ref[3] * LATE_HALF

        def block_of(g, rows):
            if g == 0:
                return sum_block(grads_ref, got_ref, rows, start, 0, LATE_ONE)
            block = sum_block(grads_ref, got_ref, rows, start, LATE_ONE, middle)
            store = store_ref[rows, :].astype(WIDE) + store_got_ref[rows, :].astype(WIDE)
            return jnp.concatenate([block, store], axis=1)

        ring_pieces(place_ref, block_of, outs)

    return whole_kernel(
        body,
        ring_shapes((LATE_ONE, LATE_TWO)),
        (place, grads, got, store_mine, store_got),
        "late_first",
        3,
        scalars=1,
        after=after,
    )


def weights_second(place, groups, after):
    ways = [way for way, _, _ in groups]
    counts = [1 + len(got) for _, _, got in groups]
    widths = [own.shape[1] for _, own, _ in groups]
    flat = [a for _, own, got in groups for a in (own, *got)]

    def body(place_ref, *refs):
        ins, outs = refs[: len(flat)], refs[len(flat) :]
        starts = [0, 0]
        first = 0
        for way, count, width in zip(ways, counts, widths):
            cols = slice(starts[way], starts[way] + width)
            starts[way] += width
            for k in range(4):
                at = (place_ref[1 - way] - k) & 3
                rows = pl.ds(pl.multiple_of(at * 48, 16), 48)
                block = ins[first][rows, :]
                for j in range(1, count):
                    block = block + ins[first + j][rows, :].astype(WIDE)
                outs[4 * way + k][:, cols] = block if k == 0 else block.astype(LOW)
            first += count

    out_shape = []
    for way in range(2):
        width = sum(w for w, at in zip(widths, ways) if at == way)
        out_shape += [wide_array(48, width)] + [low_array(48, width)] * 3
    return whole_kernel(
        body, out_shape, (place, *flat), "weights_second", 1, scalars=1, after=after
    )


def pick(pieces, index):
    chosen = pieces[0]
    for k in range(1, len(pieces)):
        chosen = jnp.where(index == k, pieces[k], chosen)
    return chosen


def weights_third(place, own, got, after):
    widths = [o.shape[1] for o in own]
    groups, total_width = len(own), sum(widths)

    def body(place_ref, *refs):
        ins, outs = refs[: 4 * groups], refs[4 * groups :]
        start = 0
        for g in range(groups):
            total = ins[g][...]
            for k in range(3):
                total = total + ins[groups + 3 * g + k][...].astype(WIDE)
            pieces = [total[k * 12 : (k + 1) * 12, :] for k in range(4)]
            cols = slice(start, start + widths[g])
            start += widths[g]
            for k in range(4):
                block = pick(pieces, (place_ref[2] - k) & 3)
                outs[k][:, cols] = block if k == 0 else block.astype(LOW)

    flat = [piece for three in got for piece in three]
    return whole_kernel(
        body,
        [wide_array(12, total_width)] + [low_array(12, total_width)] * 3,
        (place, *own, *flat),
        "weights_third",
        1,
        scalars=1,
        after=after,
    )


def weights_fourth(place, own, got):
    width = own.shape[1]

    def body(place_ref, *refs):
        total = refs[0][...]
        for k in range(3):
            total = total + refs[1 + k][...].astype(WIDE)
        pieces = [total[:6, :], total[6:, :]]
        refs[4][...] = pick(pieces, place_ref[3])
        refs[5][...] = pick(pieces, 1 - place_ref[3]).astype(LOW)

    return whole_kernel(
        body,
        [wide_array(6, width), low_array(6, width)],
        (place, own, *got),
        "weights_fourth",
        1,
        scalars=1,
    )


def to_other_core(grads):
    half = grads.shape[1] // 2
    theirs = lax.dynamic_slice_in_dim(grads, (1 - coord("core")) * half, half, 1)
    return shift(theirs, "core", 1)


def causal_bias(tokens):
    key = lax.broadcasted_iota(jnp.int32, (tokens, tokens), 0)
    query = lax.broadcasted_iota(jnp.int32, (tokens, tokens), 1)
    return jnp.where(key <= query, 0.0, MASKED)


def self_fwd_kernel(
    x_ref, wq_ref, wk_ref, wv_ref, wo_ref, q_ref, k_ref, v_ref, mixt_ref, mix_ref, lse_ref, part_ref
):
    x = x_ref[...]
    tokens = x.shape[0]
    q_ref[...] = dot(x, wq_ref[...]).astype(LOW) * jnp.asarray(SCALE, LOW)
    k_ref[...] = dot(x, wk_ref[...]).astype(LOW)
    v_ref[...] = dot(x, wv_ref[...]).astype(LOW)
    bias = causal_bias(tokens)
    lse_ref[...] = jnp.zeros_like(lse_ref)
    for pair in range(3):
        cols = slice(pair * 128, (pair + 1) * 128)
        queries, keys, values = q_ref[:, cols], k_ref[:, cols], v_ref[:, cols]
        for a in range(2):
            h = 2 * pair + a
            scores = dot(keys, first_half_lanes(queries, a), 1, 1) + bias
            top = jnp.max(scores, axis=0, keepdims=True)
            weights = jnp.exp(scores - top)
            total = jnp.sum(weights, axis=0, keepdims=True)
            mixed = dot(values, weights.astype(LOW), 0, 0)[a * HEAD_DIM : (a + 1) * HEAD_DIM, :]
            mixt_ref[h * HEAD_DIM : (h + 1) * HEAD_DIM, :] = mixed / total
            lse_ref[h : h + 1, :] = top + jnp.log(total)
    mix_ref[...] = mixt_ref[...].T.astype(LOW)
    part_ref[...] = dot(mix_ref[...], wo_ref[...]).astype(LOW)


def self_fwd(x, wq, wk, wv, wo):
    tokens = x.shape[0]
    narrow = low_array(tokens, 384)
    out_shape = [narrow, narrow, narrow, wide_array(384, tokens), narrow, wide_array(8, tokens)]
    out_shape.append(low_array(tokens, 768))
    return whole_kernel(self_fwd_kernel, out_shape, (x, wq, wk, wv, wo), "self_fwd", 3)


def self_bwd_kernel(
    e_ref,
    q_ref,
    k_ref,
    v_ref,
    mixt_ref,
    lse_ref,
    wq_ref,
    wk_ref,
    wv_ref,
    wo_ref,
    dq_ref,
    dk_ref,
    dv_ref,
    part_ref,
    dqt_s,
):
    tokens = e_ref.shape[0]
    dm = dot(e_ref[...], wo_ref[...], 1, 1).astype(LOW)
    dmt = dm.astype(WIDE).T
    bias = causal_bias(tokens)
    for pair in range(3):
        cols = slice(pair * 128, (pair + 1) * 128)
        queries, keys, values, dm_pair = q_ref[:, cols], k_ref[:, cols], v_ref[:, cols], dm[:, cols]
        dk = dv = None
        for a in range(2):
            h = 2 * pair + a
            rows = slice(h * HEAD_DIM, (h + 1) * HEAD_DIM)
            q_head = first_half_lanes(queries, a)
            dm_head = first_half_lanes(dm_pair, a)
            inner = jnp.sum(dmt[rows, :] * mixt_ref[rows, :], axis=0, keepdims=True)
            scores = dot(keys, q_head, 1, 1) + bias
            probs = jnp.exp(scores - lse_ref[h : h + 1, :])
            dp = dot(values, dm_head, 1, 1)
            ds = (probs * (dp - inner)).astype(LOW)
            dv_head = dot(probs.astype(LOW), dm_head)
            dk_head = dot(ds, q_head)
            dk = dk_head if a == 0 else dk + dk_head
            dv = dv_head if a == 0 else dv + dv_head
            dqt_s[rows, :] = dot(keys, ds, 0, 0)[a * HEAD_DIM : (a + 1) * HEAD_DIM, :] * SCALE
        dk_ref[:, cols] = dk.astype(LOW)
        dv_ref[:, cols] = dv.astype(LOW)
    dq_ref[...] = dqt_s[...].T.astype(LOW)
    part_ref[...] = (
        dot(dq_ref[...], wq_ref[...], 1, 1)
        + dot(dk_ref[...], wk_ref[...], 1, 1)
        + dot(dv_ref[...], wv_ref[...], 1, 1)
    ).astype(LOW)


def self_bwd(e_one, q, k, v, mixt, lse, wq, wk, wv, wo, after):
    tokens = e_one.shape[0]
    return whole_kernel(
        self_bwd_kernel,
        [low_array(tokens, 384)] * 3 + [low_array(tokens, 768)],
        (e_one, q, k, v, mixt, lse, wq, wk, wv, wo),
        "self_bwd",
        3,
        scratch=[pltpu.VMEM((384, tokens), WIDE)],
        after=after,
    )


def norm_back_total(mine, got, grad, normed, inv_std, gain_vec):
    tokens = mine.shape[0]

    def body(m_ref, g_ref, d_ref, n_ref, r_ref, gain_ref, out_ref, low_ref, gg_ref, gb_ref):
        total = d_ref[...] + (m_ref[...].astype(WIDE) + g_ref[...].astype(WIDE))
        kept = n_ref[...]
        scaled = total * gain_ref[...]
        centre = jnp.mean(scaled, axis=-1, keepdims=True)
        slope = jnp.mean(scaled * kept, axis=-1, keepdims=True)
        back = r_ref[...] * (scaled - centre - kept * slope)
        out_ref[...] = back
        low_ref[...] = back.astype(LOW)
        gg_ref[...] = jnp.sum(total * kept, axis=0, keepdims=True)
        gb_ref[...] = jnp.sum(total, axis=0, keepdims=True)

    out_shape = [wide_array(tokens, 768), low_array(tokens, 768)] + [wide_array(1, 768)] * 2
    back, low, gain_grad, bias_grad = whole_kernel(
        body,
        out_shape,
        (mine, got, grad, normed, inv_std, gain_vec.reshape(1, 768)),
        "norm_back",
        2,
    )
    return back, low, gain_grad[0], bias_grad[0]


def layer_norm(summed, gain_vec, bias_vec):
    row_mean = jnp.mean(summed, axis=-1, keepdims=True)
    centred = summed - row_mean
    variance = jnp.mean(centred * centred, axis=-1, keepdims=True)
    inv_std = lax.rsqrt(variance + 1e-05)
    normed = centred * inv_std
    return (normed * gain_vec + bias_vec, normed, inv_std)


def norm_back(grad_out, normed, inv_std, gain_vec):
    grad_normed = grad_out * gain_vec
    centre_term = jnp.mean(grad_normed, axis=-1, keepdims=True)
    slope_term = jnp.mean(grad_normed * normed, axis=-1, keepdims=True)
    grad_in = inv_std * (grad_normed - centre_term - normed * slope_term)
    return (grad_in, jnp.sum(grad_out * normed, axis=0), jnp.sum(grad_out, axis=0))


def shards(
    x_in,
    lengths,
    retrieved,
    datastore,
    self_wq,
    self_wk,
    self_wv,
    self_wo,
    ln1_gain,
    ln1_bias,
    cross_wq,
    cross_wk,
    cross_wv,
    cross_wo,
    ln2_gain,
    ln2_bias,
    ffn_w1,
    ffn_w2,
    ln3_gain,
    ln3_bias,
    cotangent,
):
    tokens = x_in.shape[0]
    positions = lax.iota(jnp.int32, tokens)
    place = jnp.stack([coord("y"), coord("x"), coord("z"), coord("core")]).astype(jnp.int32)
    tensor_at = lax.axis_index("tensor").astype(jnp.int32).reshape(1)

    local = project_store(datastore, cross_wk, cross_wv)
    near = [local] + shifts(local, "z")
    q_self, k_self, v_self, mixt_self, mix_self, lse_self, part = self_fwd(
        x_in, self_wq, self_wk, self_wv, self_wo
    )
    mask_one = retrieval_mask(place, retrieved, 0, (part,))
    near_a, near_b = join_near(near, (mask_one,))
    one_a, three_a = neighbours(near_a, "x")
    one_b, three_b = neighbours(near_b, "y")
    low_a, high_a, low_b, high_b = pass_on(halve(one_a, three_a, one_b, three_b, ()), "x", "y")
    kv_a, kv_b, kv_zero, states_a, states_b = join_four(
        (near_a, one_a, three_a, low_a, high_a), (near_b, one_b, three_b, low_b, high_b), ()
    )
    mask_two = retrieval_mask(place, retrieved, 1, (kv_a,))
    bias = (mask_one, mask_two)
    far_zero = shift(kv_zero, "core", 1)
    one_a, three_a = neighbours(kv_a, "y")
    one_b, three_b = neighbours(kv_b, "x")
    cut = halve(one_a, three_a, one_b, three_b, (mask_two,))
    low_a, high_a, low_b, high_b = pass_on(cut, "y", "x")

    h_one, normed_one, inv_one = layer_norm(
        x_in.astype(WIDE) + tensor_total(part), ln1_gain, ln1_bias
    )
    h_one_low = h_one.astype(LOW)
    q_cross = dot(h_one_low, cross_wq).astype(LOW) * jnp.asarray(SCALE, LOW)
    qt_cross = q_cross.T
    one_block = (((0, 0, 1024, 0),),)
    two_blocks = (((0, 0, 1024, 0),), ((0, 1024, 1024, 0),))
    state = cross_fwd(
        qt_cross,
        bias,
        (0, 4),
        (((0, 0, 1024, 0),), ((1, 0, 1024, 0),)),
        (kv_zero, far_zero),
        after=(cut[0],),
    )
    *state, kv_sides = cross_fwd(
        qt_cross,
        bias,
        (1, 3),
        (((0, 0, 512, 0), (1, 0, 512, 512)), ((2, 0, 512, 0), (3, 0, 512, 512))),
        (one_a, one_b, three_a, three_b),
        state,
        collect=True,
        after=(low_a, high_a, low_b, high_b),
    )
    far_sides = shift(kv_sides, "core", 1)
    *state, kv_two = cross_fwd(
        qt_cross,
        bias,
        (2,),
        (((0, 0, 256, 0), (1, 0, 256, 256), (2, 0, 256, 512), (3, 0, 256, 768)),),
        (low_a, high_a, low_b, high_b),
        state,
        collect=True,
    )
    far_two = shift(kv_two, "core", 1)
    state = cross_fwd(qt_cross, bias, (5, 7), two_blocks, (far_sides,), state)
    mixt_cross, mix_cross, lse_cross = cross_fwd(
        qt_cross, bias, (6,), one_block, (far_two,), state, last=True
    )
    h_two, normed_two, inv_two = layer_norm(
        h_one + tensor_total(dot(mix_cross, cross_wo)), ln2_gain, ln2_bias
    )
    h_two_low = h_two.astype(LOW)
    pre_act = dot(h_two_low, ffn_w1)
    act_low = jax.nn.gelu(pre_act).astype(LOW)
    h_three, normed_three, inv_three = layer_norm(
        h_two + tensor_total(dot(act_low, ffn_w2)), ln3_gain, ln3_bias
    )
    row_valid = (positions < lengths[0]).astype(WIDE)[:, None]
    block_out = (h_three * row_valid).astype(LOW)

    grad_out = cotangent.astype(WIDE) * row_valid
    d_three, grad_g3, grad_b3 = norm_back(grad_out, normed_three, inv_three, ln3_gain)
    e_three = d_three.astype(LOW)
    d_act = dot(e_three, ffn_w2, 1, 1)
    unused, gelu_back = jax.vjp(jax.nn.gelu, pre_act)
    d_pre = gelu_back(d_act)[0].astype(LOW)
    ffn_part = dot(d_pre, ffn_w1, 1, 1).astype(LOW)
    early_mine, early_theirs = ffn_grads(place, h_two_low, d_pre, e_three, act_low, (ffn_part,))
    early_got = shift(early_theirs, "core", 1)

    d_two, e_two, grad_g2, grad_b2 = norm_back_total(
        ffn_part, other_tensor(ffn_part), d_three, normed_two, inv_two, ln2_gain
    )
    dm_cross = dot(e_two, cross_wo, 1, 1).astype(LOW)
    dmt_cross = dm_cross.T
    inner = jnp.sum((dmt_cross.astype(WIDE) * mixt_cross).reshape(6, HEAD_DIM, tokens), axis=1)
    inner = jnp.concatenate([inner, jnp.zeros((2, tokens), WIDE)], axis=0)
    early = early_first(place, early_mine, early_got)
    sides = (qt_cross, q_cross, dmt_cross, dm_cross, lse_cross, inner)

    dqt, far = cross_bwd(
        sides,
        jnp.zeros((384, tokens), WIDE),
        bias,
        (6, 5),
        (((0, 0, 1024, 0),), ((1, 0, 1024, 0),)),
        (far_two, far_sides),
        ((0, 0, 2048),),
        after=(early[1],),
    )
    near_sums, early_yx = ring_halves(early, (dqt,))
    got_two_one = shift(far, "core", 1)
    dqt, far = cross_bwd(
        sides,
        dqt,
        bias,
        (7, 4),
        (((0, 1024, 1024, 0),), ((1, 0, 1024, 0),)),
        (far_sides, far_zero),
        ((0, 0, 2048),),
        after=(near_sums[0],),
    )
    got_three_zero = shift(far, "core", 1)
    dqt, low_a, high_a, low_b, high_b = cross_bwd(
        sides,
        dqt,
        bias,
        (2,),
        one_block,
        (kv_two,),
        tuple((0, k * 256, 256) for k in range(4)),
        adds=one_block,
        add_arrays=(got_two_one,),
    )
    low_a, low_b = shift(low_a, "y", -1), shift(low_b, "x", -1)
    high_a, high_b = shift(high_a, "y", 1), shift(high_b, "x", 1)
    dqt, own_a, own_b = cross_bwd(
        sides,
        dqt,
        bias,
        (0,),
        one_block,
        (kv_zero,),
        ((0, 0, 512), (0, 512, 512)),
        adds=(((0, 1024, 1024, 0),),),
        add_arrays=(got_three_zero,),
        after=(*early_yx[0], *early_yx[1]),
    )
    dqt, one_a, one_b, three_a, three_b = cross_bwd(
        sides,
        dqt,
        bias,
        (1, 3),
        two_blocks,
        (kv_sides,),
        ((0, 0, 512), (0, 512, 512), (1, 0, 512), (1, 512, 512)),
        adds=(((0, 1024, 1024, 0),), ((1, 0, 1024, 0),)),
        add_arrays=(got_two_one, got_three_zero),
        halves=(((0, 0, 256, 0), (1, 0, 256, 256)), ((2, 0, 256, 0), (3, 0, 256, 256))),
        half_arrays=(low_a, low_b, high_a, high_b),
    )
    got_a = [shift(one_a, "y", -1), shift(three_a, "y", 1)]
    got_b = [shift(one_b, "x", -1), shift(three_b, "x", 1)]

    blocks = store_sum_far((own_a, own_b), (got_a, got_b))
    got_a, got_b = returns(blocks[1:4], "x"), returns(blocks[5:8], "y")

    dqt_low = (dqt * SCALE).astype(LOW)
    query_part = dot(dqt_low, cross_wq, 0, 1).astype(LOW)
    d_one, e_one, grad_g1, grad_b1 = norm_back_total(
        query_part, other_tensor(query_part), d_two, normed_one, inv_one, ln1_gain
    )
    dq_self, dk_self, dv_self, part = self_bwd(
        e_one,
        q_self,
        k_self,
        v_self,
        mixt_self,
        lse_self,
        self_wq,
        self_wk,
        self_wv,
        self_wo,
        (blocks[1],),
    )
    part_got = other_tensor(part)
    input_grad = d_one + (part.astype(WIDE) + part_got.astype(WIDE))
    vectors = jnp.stack([grad_g1, grad_b1, grad_g2, grad_b2, grad_g3, grad_b3], axis=1)
    grads = [
        dot(x_in, dq_self, 0, 0),
        dot(x_in, dk_self, 0, 0),
        dot(x_in, dv_self, 0, 0),
        dot(e_one, mix_self, 0, 0),
        dot(h_one_low, dqt_low, 0, 1),
        dot(e_two, mix_cross, 0, 0),
        jnp.pad(vectors, ((0, 0), (0, 250))),
    ]
    grads = jnp.concatenate([g.astype(LOW) for g in grads], axis=1)
    late_got = to_other_core(grads)

    store_keep, store_give = store_weight_grads(place, (states_a, states_b), blocks)
    by_z = store_sum_mid((blocks[0], blocks[4]), (got_a, got_b))
    pieces = [by_z[0]] + returns(by_z[1:], "z")
    store_mine, store_send = store_finish(tensor_at, pieces, cross_wk, cross_wv)
    datastore_grad = store_mine + other_tensor(store_send).astype(WIDE)
    late = late_first(
        place, grads, late_got, store_keep, shift(store_give, "core", 1), (by_z[1],)
    )
    late_sums, late_yx = ring_halves(late)

    groups = (
        (0, late[0], late_yx[0]),
        (0, early[0], early_yx[0]),
        (1, late[5], late_yx[1]),
        (1, early[5], early_yx[1]),
    )
    blocks = weights_second(place, groups, ())
    late_xy = (returns(blocks[1:4], "x"), returns(blocks[5:8], "y"))
    last = weights_third(place, (blocks[0], blocks[4]), late_xy, (part_got,))
    keep, send = weights_fourth(place, last[0], returns(last[1:], "z"))
    got = shift(send, "core", 1).astype(WIDE)
    first = coord("core") == 0
    parts = (jnp.where(first, keep, got), jnp.where(first, got, keep))
    late_sum = jnp.concatenate(
        [c for h in parts for c in (h[:, :768], h[:, 1536:2048])], axis=1
    )
    store_sum = jnp.concatenate([h[:, 2048:2432] for h in parts], axis=1)
    grad_w1, grad_w2 = [jnp.concatenate([h[:, 768:1536], h[:, 2432:]], axis=1) for h in parts]

    part_of = lambda k: late_sum[:, k * 384 : (k + 1) * 384]
    vector = lambda k: late_sum[:, 2304 + k]
    return (
        block_out,
        input_grad,
        datastore_grad,
        part_of(0),
        part_of(1),
        part_of(2),
        part_of(3).T,
        vector(0),
        vector(1),
        part_of(4),
        store_sum[:, :384],
        store_sum[:, 384:],
        part_of(5).T,
        vector(2),
        vector(3),
        grad_w1,
        grad_w2.T,
        vector(4),
        vector(5),
    )


def solution(mesh):
    rows, columns, split = P("dp", None), P(None, "tensor"), P("tensor", None)
    norm = (P(), P())
    in_specs = (
        (rows, P("dp"), rows, rows)
        + (columns, columns, columns, split)
        + norm
        + (columns, columns, columns, split)
        + norm
        + (columns, split)
        + norm
        + (rows,)
    )
    both, turned, vector = P("dp", "tensor"), P("tensor", "dp"), P("dp")
    out_specs = (
        (rows, rows, both)
        + (both, both, both, turned)
        + (vector, vector)
        + (both, both, both, turned)
        + (vector, vector)
        + (both, turned)
        + (vector, vector)
    )
    return jax.shard_map(shards, mesh=mesh, in_specs=in_specs, out_specs=out_specs, check_vma=False)
```

```python
import functools

import jax
import jax.numpy as jnp
from jax import lax
from jax.experimental import pallas as pl
from jax.experimental.pallas import tpu as pltpu
from jax.sharding import PartitionSpec as P

LOW = jnp.bfloat16
WIDE = jnp.float32
MASKED = -1e30
HEAD_DIM = 64
SCALE = 0.125
AXES = {"y": (4, 32), "x": (4, 8), "z": (4, 2), "core": (2, 1)}
N_DP = 128
VMEM = 26 * 2**20


def dot(left, right, left_dim=1, right_dim=0):
    return lax.dot_general(
        left, right, (((left_dim,), (right_dim,)), ((), ())), preferred_element_type=WIDE
    )


def coord(axis):
    size, stride = AXES[axis]
    return (lax.axis_index("dp") // stride) % size


def shift(value, axis, step):
    size, stride = AXES[axis]
    pairs = []
    for d in range(N_DP):
        at = (d // stride) % size
        pairs.append((d, d + ((at + step) % size - at) * stride))
    return lax.ppermute(value, "dp", pairs)


def other_tensor(value):
    return lax.ppermute(value, "tensor", [(0, 1), (1, 0)])


def tensor_total(partial_value):
    mine = partial_value.astype(LOW)
    return mine.astype(WIDE) + other_tensor(mine).astype(WIDE)


def shifts(value, axis):
    return [shift(value, axis, k) for k in range(1, AXES[axis][0])]


def returns(pieces, axis):
    return [shift(piece, axis, -1 - k) for k, piece in enumerate(pieces)]


def neighbours(block, axis):
    one, three = shift(block, axis, 1), shift(block, axis, -1)
    return one, three


def whole_kernel(body, out_shape, args, name, microseconds, scratch=(), scalars=0, after=()):
    spec = lambda a: pl.BlockSpec(a.shape, lambda i: (0,) * len(a.shape))
    in_specs = [pl.BlockSpec(memory_space=pltpu.SMEM)] * scalars
    in_specs += [spec(a) for a in args[scalars:]]
    in_specs += [pl.BlockSpec(memory_space=pl.ANY)] * len(after)
    out_specs = [spec(a) for a in out_shape] if isinstance(out_shape, list) else spec(out_shape)
    used, skipped = len(args), len(args) + len(after)

    def kernel(*refs):
        body(*refs[:used], *refs[skipped:])

    return pl.pallas_call(
        kernel,
        out_shape=out_shape,
        grid=(1,),
        in_specs=in_specs,
        out_specs=out_specs,
        scratch_shapes=list(scratch),
        compiler_params=pltpu.CompilerParams(vmem_limit_bytes=VMEM),
        cost_estimate=cost(microseconds, 1e6),
        name=name,
    )(*args, *after)


def cost(microseconds, moved):
    return pl.CostEstimate(
        flops=int(microseconds * 5e9), bytes_accessed=int(moved), transcendentals=0
    )


def low_array(*shape):
    return jax.ShapeDtypeStruct(shape, LOW)


def wide_array(*shape):
    return jax.ShapeDtypeStruct(shape, WIDE)


def first_half_rows(pair, which):
    row = lax.broadcasted_iota(jnp.int32, pair.shape, 0)
    return jnp.where((row < HEAD_DIM) == (which == 0), pair, jnp.zeros_like(pair))


def first_half_lanes(pair, which):
    lane = lax.broadcasted_iota(jnp.int32, pair.shape, 1)
    return jnp.where((lane < HEAD_DIM) == (which == 0), pair, jnp.zeros_like(pair))


def project_store(datastore, wk, wv):
    def body(s_ref, k_ref, v_ref, out_ref):
        out_ref[:, :384] = dot(s_ref[...], k_ref[...]).astype(LOW)
        out_ref[:, 384:768] = dot(s_ref[...], v_ref[...]).astype(LOW)
        out_ref[:, 768:] = s_ref[...]

    return whole_kernel(body, low_array(64, 1536), (datastore, wk, wv), "project_store", 1)


def join_near(pieces, after):
    def body(*refs):
        for k in range(4):
            refs[4][k * 32 : (k + 1) * 32, :] = refs[k][:32, :]
            refs[5][k * 32 : (k + 1) * 32, :] = refs[k][32:, :]

    return whole_kernel(body, [low_array(128, 1536)] * 2, pieces, "join_near", 1, after=after)


def halve(one_a, three_a, one_b, three_b, after):
    rows, width = one_a.shape
    half = rows // 2

    def body(*refs):
        for k in range(4):
            refs[4 + k][...] = refs[k][:half, :] if k % 2 == 0 else refs[k][half:, :]

    return whole_kernel(
        body, [low_array(half, width)] * 4, (one_a, three_a, one_b, three_b), "halve", 1, after=after
    )


def pass_on(halves, axis_a, axis_b):
    low_a, high_a, low_b, high_b = halves
    return (
        shift(low_a, axis_a, 1),
        shift(high_a, axis_a, -1),
        shift(low_b, axis_b, 1),
        shift(high_b, axis_b, -1),
    )


def join_four(pieces_a, pieces_b, after):
    def body(*refs):
        ins, outs = refs[:10], refs[10:]
        for g in range(2):
            own, one, three, low, high = ins[5 * g : 5 * g + 5]
            for ref, at in ((own, 0), (one, 128), (low, 256), (high, 320), (three, 384)):
                rows = slice(at, at + ref.shape[0])
                outs[g][rows, :] = ref[:, :768]
                outs[2][g * 512 + at : g * 512 + at + ref.shape[0], :] = ref[:, :768]
                outs[3 + g][rows, :] = ref[:, 768:]

    out_shape = [low_array(512, 768)] * 2 + [low_array(1024, 768)] + [low_array(512, 768)] * 2
    return whole_kernel(body, out_shape, (*pieces_a, *pieces_b), "join_four", 2, after=after)


def mask_body(place_ref, picks_ref, out_ref, high_s, low_s, count_s):
    picks = picks_ref[...]
    core = (place_ref[3] - (picks >> 6)) & 1
    at_z = (place_ref[2] - (picks >> 7)) & 3
    at_x = (place_ref[1] - (picks >> 9)) & 3
    at_y = (place_ref[0] - (picks >> 11)) & 3
    group = (picks >> 5) & 1
    chunk = jnp.where(group == 0, at_y, at_x)
    inside = jnp.where(group == 0, at_x, at_y)
    high_s[...] = (core << 5) | (chunk << 3) | (group << 2) | inside
    low_s[...] = (at_z << 5) | (picks & 31)
    rows, k_top = picks_ref.shape

    def count(t, carry):
        high = high_s[pl.ds(t, 1), :]
        low = low_s[pl.ds(t, 1), :]
        is_high = lax.broadcasted_iota(jnp.int32, (64, k_top), 0) == high
        is_low = lax.broadcasted_iota(jnp.int32, (128, k_top), 0) == low
        count_s[pl.ds(pl.multiple_of(t * 64, 64), 64), :] = dot(
            jnp.where(is_high, 1.0, 0.0).astype(jnp.float8_e4m3fn),
            jnp.where(is_low, 1.0, 0.0).astype(jnp.float8_e4m3fn),
            1,
            1,
        )
        return carry

    lax.fori_loop(0, rows, count, 0, unroll=8)

    def turn(h, carry):
        block = count_s[pl.ds(h, rows, stride=64), :]
        bias = jnp.where(block.T > 0.5, 0.0, MASKED)
        out_ref[pl.ds(pl.multiple_of(h * 128, 128), 128), :] = bias.astype(LOW)
        return carry

    lax.fori_loop(0, 64, turn, 0, unroll=2)


def retrieval_mask(place, picks, part, after):
    tokens, k_top = picks.shape
    rows = tokens // 2

    def kernel(place_ref, picks_ref, *refs):
        mask_body(place_ref, picks_ref, *refs[len(after) :])

    return pl.pallas_call(
        kernel,
        out_shape=low_array(8192, rows),
        grid=(1,),
        in_specs=[
            pl.BlockSpec(memory_space=pltpu.SMEM),
            pl.BlockSpec((rows, k_top), lambda i: (part, 0)),
        ]
        + anywhere(len(after)),
        out_specs=pl.BlockSpec((8192, rows), lambda i: (0, 0)),
        scratch_shapes=[
            pltpu.VMEM((rows, k_top), jnp.int32),
            pltpu.VMEM((rows, k_top), jnp.int32),
            pltpu.VMEM((rows * 64, 128), WIDE),
        ],
        compiler_params=pltpu.CompilerParams(vmem_limit_bytes=VMEM),
        cost_estimate=cost(17, 3e6),
        name="retrieval_mask",
    )(place, picks, *after)


def load_blocks(blocks, refs, into, sems, column):
    for i, pieces in enumerate(blocks):
        for operand, row, rows, to in pieces:
            pltpu.make_async_copy(
                refs[operand].at[pl.ds(row, rows)],
                into.at[i, pl.ds(to, rows)],
                sems.at[i, column],
            ).start()

    def wait(i):
        pltpu.make_async_copy(into.at[i], into.at[i], sems.at[i, column]).wait()

    return wait


def load_masks(chunks, bias_refs, into, sems, column):
    for i, chunk in enumerate(chunks):
        for j in range(2):
            pltpu.make_async_copy(
                bias_refs[j].at[pl.ds(chunk * 1024, 1024)],
                into.at[i, :, pl.ds(j * 128, 128)],
                sems.at[i, column],
            ).start()

    def wait(i):
        pltpu.make_async_copy(into.at[i], into.at[i], sems.at[i, column]).wait()

    return wait


def in_vmem(count):
    return [pl.BlockSpec(memory_space=pltpu.VMEM)] * count


def anywhere(count):
    return [pl.BlockSpec(memory_space=pl.ANY)] * count


def cross_fwd_body(chunks, blocks, counts, first, last, collect, *refs):
    n = len(chunks)
    n_arrays, n_after = counts
    qt_ref, refs = refs[0], refs[1:]
    if not first:
        state, refs = refs[:3], refs[3:]
    bias_refs, arrays, refs = refs[:2], refs[2 : 2 + n_arrays], refs[2 + n_arrays + n_after :]
    outs, refs = refs[:3], refs[3:]
    if collect:
        collected, refs = refs[0], refs[1:]
    kv_s, bias_s, sems, out_sem = refs[:4]
    if last:
        mixt_ref, mix_ref, lse_ref = outs
        acc, top_s, sum_s = refs[4:]
    else:
        acc, top_s, sum_s = outs
    wait_kv = load_blocks(blocks, arrays, kv_s, sems, 0)
    wait_bias = load_masks(chunks, bias_refs, bias_s, sems, 1)
    if first:
        acc[...] = jnp.zeros_like(acc)
        top_s[...] = jnp.full_like(top_s, MASKED)
        sum_s[...] = jnp.zeros_like(sum_s)
    else:
        acc[...] = state[0][...]
        top_s[...] = state[1][...]
        sum_s[...] = state[2][...]

    def step(i, carry):
        wait_kv(i)
        if collect:
            rows = pl.ds(pl.multiple_of(i * 1024, 1024), 1024)
            pltpu.make_async_copy(kv_s.at[i], collected.at[rows], out_sem).start()
        wait_bias(i)
        bias = bias_s[i].astype(WIDE)
        for pair in range(3):
            cols = slice(pair * 128, (pair + 1) * 128)
            keys = kv_s[i, :, cols]
            values = kv_s[i, :, 384 + pair * 128 : 512 + pair * 128]
            queries = qt_ref[cols, :]
            for a in range(2):
                h = 2 * pair + a
                rows = slice(h * HEAD_DIM, (h + 1) * HEAD_DIM)
                scores = dot(keys, first_half_rows(queries, a)) + bias
                old = top_s[h : h + 1, :]
                top = jnp.maximum(old, jnp.max(scores, axis=0, keepdims=True))
                fade = jnp.exp(old - top)
                weights = jnp.exp(scores - top)
                sum_s[h : h + 1, :] = sum_s[h : h + 1, :] * fade + jnp.sum(
                    weights, axis=0, keepdims=True
                )
                top_s[h : h + 1, :] = top
                mixed = dot(values, weights.astype(LOW), 0, 0)
                acc[rows, :] = acc[rows, :] * fade + mixed[a * HEAD_DIM : (a + 1) * HEAD_DIM, :]
        return carry

    lax.fori_loop(0, n, step, 0)
    if last:
        for h in range(6):
            rows = slice(h * HEAD_DIM, (h + 1) * HEAD_DIM)
            acc[rows, :] = acc[rows, :] / sum_s[h : h + 1, :]
        mixt_ref[...] = acc[...]
        mix_ref[...] = acc[...].T.astype(LOW)
        lse_ref[...] = top_s[...] + jnp.log(jnp.maximum(sum_s[...], 1e-30))
    if collect:
        pltpu.make_async_copy(collected, collected, out_sem).wait()


def cross_fwd(
    qt, bias, chunks, blocks, arrays, state=None, last=False, collect=False, after=()
):
    tokens, n = qt.shape[1], len(chunks)
    kept = [wide_array(384, tokens), wide_array(8, tokens), wide_array(8, tokens)]
    scratch = [
        pltpu.VMEM((n, 1024, 768), LOW),
        pltpu.VMEM((n, 1024, tokens), LOW),
        pltpu.SemaphoreType.DMA((n, 2)),
        pltpu.SemaphoreType.DMA,
    ]
    if last:
        out_shape = [kept[0], low_array(tokens, 384), kept[1]]
        scratch += [pltpu.VMEM(a.shape, WIDE) for a in kept]
    else:
        out_shape = list(kept)
    out_specs = in_vmem(3)
    if collect:
        out_shape.append(low_array(n * 1024, 768))
        out_specs += anywhere(1)
    given = (qt,) + (() if state is None else tuple(state))
    return pl.pallas_call(
        functools.partial(
            cross_fwd_body,
            chunks,
            blocks,
            (len(arrays), len(after)),
            state is None,
            last,
            collect,
        ),
        out_shape=out_shape,
        in_specs=in_vmem(len(given)) + anywhere(2 + len(arrays) + len(after)),
        out_specs=out_specs,
        scratch_shapes=scratch,
        compiler_params=pltpu.CompilerParams(vmem_limit_bytes=VMEM),
        cost_estimate=cost(4 * n, 2e6 * n),
        name="cross_fwd",
    )(*given, *bias, *arrays, *after)


def cross_bwd_body(chunks, blocks, adds, halves, pieces, counts, *refs):
    n = len(chunks)
    n_arrays, n_adds, n_halves, n_after = counts
    qt_ref, q_ref, dmt_ref, dm_ref, lse_ref, inner_ref, dq_in = refs[:7]
    bias_refs, refs = refs[7:9], refs[9:]
    arrays, refs = refs[:n_arrays], refs[n_arrays:]
    add_refs, refs = refs[:n_adds], refs[n_adds:]
    half_refs, refs = refs[:n_halves], refs[n_halves + n_after :]
    dq_ref, outs, refs = refs[0], refs[1 : 1 + len(pieces)], refs[1 + len(pieces) :]
    kv_s, bias_s, out_s, sems, out_sems, refs = *refs[:5], refs[5:]
    wait_kv = load_blocks(blocks, arrays, kv_s, sems, 0)
    wait_bias = load_masks(chunks, bias_refs, bias_s, sems, 1)
    if adds:
        add_s = refs[0]
        wait_add = load_blocks(adds, add_refs, add_s, sems, 2)
    if halves:
        half_s = refs[1]
        wait_half = load_blocks(halves, half_refs, half_s, sems, 3)
        for i in range(n):
            wait_add(i)
            wait_half(i)
            for g in range(2):
                at = slice(g * 512 + i * 256, g * 512 + i * 256 + 256)
                both = add_s[i, at, :].astype(WIDE) + half_s[i, g * 256 : g * 256 + 256, :].astype(
                    WIDE
                )
                add_s[i, at, :] = both.astype(LOW)
    dq_ref[...] = dq_in[...]

    def step(i, carry):
        wait_kv(i)
        wait_bias(i)
        if adds and not halves:
            wait_add(i)
        bias = bias_s[i].astype(WIDE)
        for pair in range(3):
            cols = slice(pair * 128, (pair + 1) * 128)
            v_cols = slice(384 + pair * 128, 512 + pair * 128)
            keys, values = kv_s[i, :, cols], kv_s[i, :, v_cols]
            dk = dv = None
            for a in range(2):
                h = 2 * pair + a
                rows = slice(h * HEAD_DIM, (h + 1) * HEAD_DIM)
                scores = dot(keys, first_half_rows(qt_ref[cols, :], a)) + bias
                probs = jnp.exp(scores - lse_ref[h : h + 1, :])
                dp = dot(values, first_half_rows(dmt_ref[cols, :], a))
                ds = (probs * (dp - inner_ref[h : h + 1, :])).astype(LOW)
                dv_head = dot(probs.astype(LOW), first_half_lanes(dm_ref[:, cols], a))
                dk_head = dot(ds, first_half_lanes(q_ref[:, cols], a))
                dk = dk_head if a == 0 else dk + dk_head
                dv = dv_head if a == 0 else dv + dv_head
                dq = dot(keys, ds, 0, 0)
                dq_ref[rows, :] += dq[a * HEAD_DIM : (a + 1) * HEAD_DIM, :]
            if adds:
                dk = dk + add_s[i, :, cols].astype(WIDE)
                dv = dv + add_s[i, :, v_cols].astype(WIDE)
            out_s[i, :, cols] = dk.astype(LOW)
            out_s[i, :, v_cols] = dv.astype(LOW)
        return carry

    if n == 1:
        step(0, 0)
    else:
        lax.fori_loop(0, n, step, 0)
    copies = []
    for j, (i, row, rows) in enumerate(pieces):
        if rows > 1024:
            for b in range(n):
                copies.append(
                    pltpu.make_async_copy(
                        out_s.at[b], outs[j].at[pl.ds(b * 1024, 1024)], out_sems.at[b]
                    )
                )
        else:
            copies.append(
                pltpu.make_async_copy(out_s.at[i, pl.ds(row, rows)], outs[j], out_sems.at[j])
            )
    for copy in copies:
        copy.start()
    for copy in copies:
        copy.wait()


def cross_bwd(
    sides, dq, bias, chunks, blocks, arrays, pieces, adds=(), add_arrays=(), halves=(),
    half_arrays=(), after=(),
):
    tokens, n = dq.shape[1], len(chunks)
    scratch = [
        pltpu.VMEM((n, 1024, 768), LOW),
        pltpu.VMEM((n, 1024, tokens), LOW),
        pltpu.VMEM((n, 1024, 768), LOW),
        pltpu.SemaphoreType.DMA((n, 4)),
        pltpu.SemaphoreType.DMA((max(n, len(pieces)),)),
    ]
    if adds:
        scratch.append(pltpu.VMEM((n, 1024, 768), LOW))
    if halves:
        scratch.append(pltpu.VMEM((n, 512, 768), LOW))
    counts = (len(arrays), len(add_arrays), len(half_arrays), len(after))
    return pl.pallas_call(
        functools.partial(cross_bwd_body, chunks, blocks, adds, halves, pieces, counts),
        out_shape=[wide_array(384, tokens)] + [low_array(rows, 768) for _, _, rows in pieces],
        in_specs=in_vmem(7) + anywhere(2 + sum(counts)),
        out_specs=in_vmem(1) + anywhere(len(pieces)),
        scratch_shapes=scratch,
        compiler_params=pltpu.CompilerParams(vmem_limit_bytes=VMEM),
        cost_estimate=cost(4.5 * n, 4e6 * n),
        name="cross_bwd",
    )(*sides, dq, *bias, *arrays, *add_arrays, *half_arrays, *after)


def store_sum_far(own, got):
    def body(*refs):
        ins, outs = refs[:6], refs[6:]
        for g in range(2):
            total = ins[g][...].astype(WIDE)
            for k in range(2):
                total = total + ins[2 + 2 * g + k][...].astype(WIDE)
            for k in range(4):
                outs[4 * g + k][...] = total[k * 128 : (k + 1) * 128, :].astype(LOW)

    return whole_kernel(
        body, [low_array(128, 768)] * 8, (*own, *got[0], *got[1]), "store_sum_far", 2
    )


def store_weight_grads(place, states, blocks):
    def body(place_ref, *refs):
        sum_s = refs[12]
        for c in range(0, 768, 256):
            total = None
            for g in range(2):
                for k in range(4):
                    part = dot(
                        refs[g][k * 128 : (k + 1) * 128, c : c + 256], refs[2 + 4 * g + k][...], 0, 0
                    )
                    total = part if total is None else total + part
            sum_s[c : c + 256, :] = total.astype(LOW)
        mine = pl.multiple_of(place_ref[3] * 384, 128)
        theirs = pl.multiple_of((1 - place_ref[3]) * 384, 128)
        refs[10][...] = sum_s[:, pl.ds(mine, 384)]
        refs[11][...] = sum_s[:, pl.ds(theirs, 384)]

    return whole_kernel(
        body,
        [low_array(768, 384)] * 2,
        (place, *states, *blocks),
        "store_weight_grads",
        3,
        scratch=[pltpu.VMEM((768, 768), LOW)],
        scalars=1,
    )


def store_sum_mid(own, got):
    def body(*refs):
        ins, outs = refs[:8], refs[8:]
        for g in range(2):
            total = ins[g][...].astype(WIDE)
            for k in range(3):
                total = total + ins[2 + 3 * g + k][...].astype(WIDE)
            for k in range(4):
                outs[k][g * 32 : (g + 1) * 32, :] = total[k * 32 : (k + 1) * 32, :].astype(LOW)

    return whole_kernel(body, [low_array(64, 768)] * 4, (*own, *got[0], *got[1]), "store_sum_mid", 1)


def store_finish(tensor_at, pieces, wk, wv):
    def body(at_ref, *refs):
        total = refs[0][...].astype(WIDE)
        for k in range(1, 4):
            total = total + refs[k][...].astype(WIDE)
        total = total.astype(LOW)
        part = refs[8]
        part[...] = dot(total[:, :384], refs[4][...], 1, 1) + dot(total[:, 384:], refs[5][...], 1, 1)
        mine = pl.multiple_of(at_ref[0] * 384, 128)
        theirs = pl.multiple_of((1 - at_ref[0]) * 384, 128)
        refs[6][...] = part[:, pl.ds(mine, 384)]
        refs[7][...] = part[:, pl.ds(theirs, 384)].astype(LOW)

    return whole_kernel(
        body,
        [wide_array(64, 384), low_array(64, 384)],
        (tensor_at, *pieces, wk, wv),
        "store_finish",
        1,
        scratch=[pltpu.VMEM((64, 768), WIDE)],
        scalars=1,
    )


def sum_block(grads_ref, got_ref, rows, start, col, width):
    cols = pl.ds(pl.multiple_of(start + col, 128), width)
    return grads_ref[rows, cols].astype(WIDE) + got_ref[rows, col : col + width].astype(WIDE)


def ffn_grads(place, h_two, d_pre, e_three, act, after):
    def body(place_ref, h_ref, d_ref, e_ref, a_ref, mine_ref, theirs_ref):
        first = place_ref[3] == 0
        for left, right, is_mine in ((h_ref, d_ref, first), (e_ref, a_ref, jnp.logical_not(first))):
            for c in range(0, 1536, 512):
                part = dot(left[...], right[:, c : c + 512], 0, 0).astype(LOW)

                @pl.when(is_mine)
                def keep():
                    mine_ref[:, c : c + 512] = part

                @pl.when(jnp.logical_not(is_mine))
                def give():
                    theirs_ref[:, c : c + 512] = part

    return whole_kernel(
        body,
        [low_array(768, 1536)] * 2,
        (place, h_two, d_pre, e_three, act),
        "ffn_grads",
        3,
        scalars=1,
        after=after,
    )


def ring_pieces(place_ref, block_of, outs):
    for k in range(4):
        at_y = ((place_ref[0] - k) & 3) * 192
        at_x = ((place_ref[1] - k) & 3) * 48
        for part in range(4):
            to = slice(part * 48, part * 48 + 48)
            half_to = slice(part % 2 * 48, part % 2 * 48 + 48)
            for g in range(2):
                row = at_y + part * 48 if g == 0 else part * 192 + at_x
                block = block_of(g, pl.ds(pl.multiple_of(row, 16), 48))
                if k == 0:
                    outs[5 * g][to, :] = block
                elif k == 2:
                    outs[5 * g + 3 + part // 2][half_to, :] = block.astype(LOW)
                else:
                    outs[5 * g + (k + 1) // 2][to, :] = block.astype(LOW)


def ring_shapes(widths):
    shapes = []
    for width in widths:
        shapes += [wide_array(192, width)] + [low_array(192, width)] * 2
        shapes += [low_array(96, width)] * 2
    return shapes


def ring_halves(pieces, after=()):
    halves = (
        shift(pieces[3], "y", -1),
        shift(pieces[4], "y", 1),
        shift(pieces[8], "x", -1),
        shift(pieces[9], "x", 1),
    )
    sums = ring_middle((pieces[1], pieces[2], pieces[6], pieces[7]), halves, after)
    return sums, (
        (shift(sums[0], "y", -1), shift(sums[1], "y", 1)),
        (shift(sums[2], "x", -1), shift(sums[3], "x", 1)),
    )


def early_first(place, grads, got, after):
    width = grads.shape[1] // 2

    def body(place_ref, grads_ref, got_ref, *outs):
        def block_of(g, rows):
            cols = slice(g * width, (g + 1) * width)
            return grads_ref[rows, cols].astype(WIDE) + got_ref[rows, cols].astype(WIDE)

        ring_pieces(place_ref, block_of, outs)

    shapes = ring_shapes((width, width))
    return whole_kernel(
        body, shapes, (place, grads, got), "early_first", 3, scalars=1, after=after
    )


def ring_middle(sides, got, after):
    def body(*refs):
        for g in range(2):
            for j in range(2):
                ref, half, out = refs[2 * g + j], refs[4 + 2 * g + j], refs[8 + 2 * g + j]
                summed, kept = (slice(0, 96), slice(96, 192))[:: 1 - 2 * j]
                both = ref[summed, :].astype(WIDE) + half[...].astype(WIDE)
                out[summed, :] = both.astype(LOW)
                out[kept, :] = ref[kept, :]

    return whole_kernel(
        body,
        [low_array(*side.shape) for side in sides],
        (*sides, *got),
        "ring_middle",
        1,
        after=after,
    )


LATE_ONE, LATE_TWO = 768, 896
LATE_HALF = 1280


def late_first(place, grads, got, store_mine, store_got, after):
    middle = LATE_HALF - LATE_ONE

    def body(place_ref, grads_ref, got_ref, store_ref, store_got_ref, *outs):
        start = place_ref[3] * LATE_HALF

        def block_of(g, rows):
            if g == 0:
                return sum_block(grads_ref, got_ref, rows, start, 0, LATE_ONE)
            block = sum_block(grads_ref, got_ref, rows, start, LATE_ONE, middle)
            store = store_ref[rows, :].astype(WIDE) + store_got_ref[rows, :].astype(WIDE)
            return jnp.concatenate([block, store], axis=1)

        ring_pieces(place_ref, block_of, outs)

    return whole_kernel(
        body,
        ring_shapes((LATE_ONE, LATE_TWO)),
        (place, grads, got, store_mine, store_got),
        "late_first",
        3,
        scalars=1,
        after=after,
    )


def weights_second(place, groups, after):
    ways = [way for way, _, _ in groups]
    counts = [1 + len(got) for _, _, got in groups]
    widths = [own.shape[1] for _, own, _ in groups]
    flat = [a for _, own, got in groups for a in (own, *got)]

    def body(place_ref, *refs):
        ins, outs = refs[: len(flat)], refs[len(flat) :]
        starts = [0, 0]
        first = 0
        for way, count, width in zip(ways, counts, widths):
            cols = slice(starts[way], starts[way] + width)
            starts[way] += width
            for k in range(4):
                at = (place_ref[1 - way] - k) & 3
                rows = pl.ds(pl.multiple_of(at * 48, 16), 48)
                block = ins[first][rows, :]
                for j in range(1, count):
                    block = block + ins[first + j][rows, :].astype(WIDE)
                outs[4 * way + k][:, cols] = block if k == 0 else block.astype(LOW)
            first += count

    out_shape = []
    for way in range(2):
        width = sum(w for w, at in zip(widths, ways) if at == way)
        out_shape += [wide_array(48, width)] + [low_array(48, width)] * 3
    return whole_kernel(
        body, out_shape, (place, *flat), "weights_second", 1, scalars=1, after=after
    )


def pick(pieces, index):
    chosen = pieces[0]
    for k in range(1, len(pieces)):
        chosen = jnp.where(index == k, pieces[k], chosen)
    return chosen


def weights_third(place, own, got, after):
    widths = [o.shape[1] for o in own]
    groups, total_width = len(own), sum(widths)

    def body(place_ref, *refs):
        ins, outs = refs[: 4 * groups], refs[4 * groups :]
        start = 0
        for g in range(groups):
            total = ins[g][...]
            for k in range(3):
                total = total + ins[groups + 3 * g + k][...].astype(WIDE)
            pieces = [total[k * 12 : (k + 1) * 12, :] for k in range(4)]
            cols = slice(start, start + widths[g])
            start += widths[g]
            for k in range(4):
                block = pick(pieces, (place_ref[2] - k) & 3)
                outs[k][:, cols] = block if k == 0 else block.astype(LOW)

    flat = [piece for three in got for piece in three]
    return whole_kernel(
        body,
        [wide_array(12, total_width)] + [low_array(12, total_width)] * 3,
        (place, *own, *flat),
        "weights_third",
        1,
        scalars=1,
        after=after,
    )


def weights_fourth(place, own, got):
    width = own.shape[1]

    def body(place_ref, *refs):
        total = refs[0][...]
        for k in range(3):
            total = total + refs[1 + k][...].astype(WIDE)
        pieces = [total[:6, :], total[6:, :]]
        refs[4][...] = pick(pieces, place_ref[3])
        refs[5][...] = pick(pieces, 1 - place_ref[3]).astype(LOW)

    return whole_kernel(
        body,
        [wide_array(6, width), low_array(6, width)],
        (place, own, *got),
        "weights_fourth",
        1,
        scalars=1,
    )


def to_other_core(grads):
    half = grads.shape[1] // 2
    theirs = lax.dynamic_slice_in_dim(grads, (1 - coord("core")) * half, half, 1)
    return shift(theirs, "core", 1)


def causal_bias(tokens):
    key = lax.broadcasted_iota(jnp.int32, (tokens, tokens), 0)
    query = lax.broadcasted_iota(jnp.int32, (tokens, tokens), 1)
    return jnp.where(key <= query, 0.0, MASKED)


def self_fwd_kernel(
    x_ref, wq_ref, wk_ref, wv_ref, wo_ref, q_ref, k_ref, v_ref, mixt_ref, mix_ref, lse_ref, part_ref
):
    x = x_ref[...]
    tokens = x.shape[0]
    q_ref[...] = dot(x, wq_ref[...]).astype(LOW) * jnp.asarray(SCALE, LOW)
    k_ref[...] = dot(x, wk_ref[...]).astype(LOW)
    v_ref[...] = dot(x, wv_ref[...]).astype(LOW)
    bias = causal_bias(tokens)
    lse_ref[...] = jnp.zeros_like(lse_ref)
    for pair in range(3):
        cols = slice(pair * 128, (pair + 1) * 128)
        queries, keys, values = q_ref[:, cols], k_ref[:, cols], v_ref[:, cols]
        for a in range(2):
            h = 2 * pair + a
            scores = dot(keys, first_half_lanes(queries, a), 1, 1) + bias
            top = jnp.max(scores, axis=0, keepdims=True)
            weights = jnp.exp(scores - top)
            total = jnp.sum(weights, axis=0, keepdims=True)
            mixed = dot(values, weights.astype(LOW), 0, 0)[a * HEAD_DIM : (a + 1) * HEAD_DIM, :]
            mixt_ref[h * HEAD_DIM : (h + 1) * HEAD_DIM, :] = mixed / total
            lse_ref[h : h + 1, :] = top + jnp.log(total)
    mix_ref[...] = mixt_ref[...].T.astype(LOW)
    part_ref[...] = dot(mix_ref[...], wo_ref[...]).astype(LOW)


def self_fwd(x, wq, wk, wv, wo):
    tokens = x.shape[0]
    narrow = low_array(tokens, 384)
    out_shape = [narrow, narrow, narrow, wide_array(384, tokens), narrow, wide_array(8, tokens)]
    out_shape.append(low_array(tokens, 768))
    return whole_kernel(self_fwd_kernel, out_shape, (x, wq, wk, wv, wo), "self_fwd", 3)


def self_bwd_kernel(
    e_ref,
    q_ref,
    k_ref,
    v_ref,
    mixt_ref,
    lse_ref,
    wq_ref,
    wk_ref,
    wv_ref,
    wo_ref,
    dq_ref,
    dk_ref,
    dv_ref,
    part_ref,
    dqt_s,
):
    tokens = e_ref.shape[0]
    dm = dot(e_ref[...], wo_ref[...], 1, 1).astype(LOW)
    dmt = dm.astype(WIDE).T
    bias = causal_bias(tokens)
    for pair in range(3):
        cols = slice(pair * 128, (pair + 1) * 128)
        queries, keys, values, dm_pair = q_ref[:, cols], k_ref[:, cols], v_ref[:, cols], dm[:, cols]
        dk = dv = None
        for a in range(2):
            h = 2 * pair + a
            rows = slice(h * HEAD_DIM, (h + 1) * HEAD_DIM)
            q_head = first_half_lanes(queries, a)
            dm_head = first_half_lanes(dm_pair, a)
            inner = jnp.sum(dmt[rows, :] * mixt_ref[rows, :], axis=0, keepdims=True)
            scores = dot(keys, q_head, 1, 1) + bias
            probs = jnp.exp(scores - lse_ref[h : h + 1, :])
            dp = dot(values, dm_head, 1, 1)
            ds = (probs * (dp - inner)).astype(LOW)
            dv_head = dot(probs.astype(LOW), dm_head)
            dk_head = dot(ds, q_head)
            dk = dk_head if a == 0 else dk + dk_head
            dv = dv_head if a == 0 else dv + dv_head
            dqt_s[rows, :] = dot(keys, ds, 0, 0)[a * HEAD_DIM : (a + 1) * HEAD_DIM, :] * SCALE
        dk_ref[:, cols] = dk.astype(LOW)
        dv_ref[:, cols] = dv.astype(LOW)
    dq_ref[...] = dqt_s[...].T.astype(LOW)
    part_ref[...] = (
        dot(dq_ref[...], wq_ref[...], 1, 1)
        + dot(dk_ref[...], wk_ref[...], 1, 1)
        + dot(dv_ref[...], wv_ref[...], 1, 1)
    ).astype(LOW)


def self_bwd(e_one, q, k, v, mixt, lse, wq, wk, wv, wo, after):
    tokens = e_one.shape[0]
    return whole_kernel(
        self_bwd_kernel,
        [low_array(tokens, 384)] * 3 + [low_array(tokens, 768)],
        (e_one, q, k, v, mixt, lse, wq, wk, wv, wo),
        "self_bwd",
        3,
        scratch=[pltpu.VMEM((384, tokens), WIDE)],
        after=after,
    )


def norm_back_total(mine, got, grad, normed, inv_std, gain_vec):
    tokens = mine.shape[0]

    def body(m_ref, g_ref, d_ref, n_ref, r_ref, gain_ref, out_ref, low_ref, gg_ref, gb_ref):
        total = d_ref[...] + (m_ref[...].astype(WIDE) + g_ref[...].astype(WIDE))
        kept = n_ref[...]
        scaled = total * gain_ref[...]
        centre = jnp.mean(scaled, axis=-1, keepdims=True)
        slope = jnp.mean(scaled * kept, axis=-1, keepdims=True)
        back = r_ref[...] * (scaled - centre - kept * slope)
        out_ref[...] = back
        low_ref[...] = back.astype(LOW)
        gg_ref[...] = jnp.sum(total * kept, axis=0, keepdims=True)
        gb_ref[...] = jnp.sum(total, axis=0, keepdims=True)

    out_shape = [wide_array(tokens, 768), low_array(tokens, 768)] + [wide_array(1, 768)] * 2
    back, low, gain_grad, bias_grad = whole_kernel(
        body,
        out_shape,
        (mine, got, grad, normed, inv_std, gain_vec.reshape(1, 768)),
        "norm_back",
        2,
    )
    return back, low, gain_grad[0], bias_grad[0]


def layer_norm(summed, gain_vec, bias_vec):
    row_mean = jnp.mean(summed, axis=-1, keepdims=True)
    centred = summed - row_mean
    variance = jnp.mean(centred * centred, axis=-1, keepdims=True)
    inv_std = lax.rsqrt(variance + 1e-05)
    normed = centred * inv_std
    return (normed * gain_vec + bias_vec, normed, inv_std)


def norm_back(grad_out, normed, inv_std, gain_vec):
    grad_normed = grad_out * gain_vec
    centre_term = jnp.mean(grad_normed, axis=-1, keepdims=True)
    slope_term = jnp.mean(grad_normed * normed, axis=-1, keepdims=True)
    grad_in = inv_std * (grad_normed - centre_term - normed * slope_term)
    return (grad_in, jnp.sum(grad_out * normed, axis=0), jnp.sum(grad_out, axis=0))


def shards(
    x_in,
    lengths,
    retrieved,
    datastore,
    self_wq,
    self_wk,
    self_wv,
    self_wo,
    ln1_gain,
    ln1_bias,
    cross_wq,
    cross_wk,
    cross_wv,
    cross_wo,
    ln2_gain,
    ln2_bias,
    ffn_w1,
    ffn_w2,
    ln3_gain,
    ln3_bias,
    cotangent,
):
    tokens = x_in.shape[0]
    positions = lax.iota(jnp.int32, tokens)
    place = jnp.stack([coord("y"), coord("x"), coord("z"), coord("core")]).astype(jnp.int32)
    tensor_at = lax.axis_index("tensor").astype(jnp.int32).reshape(1)

    local = project_store(datastore, cross_wk, cross_wv)
    near = [local] + shifts(local, "z")
    q_self, k_self, v_self, mixt_self, mix_self, lse_self, part = self_fwd(
        x_in, self_wq, self_wk, self_wv, self_wo
    )
    mask_one = retrieval_mask(place, retrieved, 0, (part,))
    near_a, near_b = join_near(near, (mask_one,))
    one_a, three_a = neighbours(near_a, "x")
    one_b, three_b = neighbours(near_b, "y")
    low_a, high_a, low_b, high_b = pass_on(halve(one_a, three_a, one_b, three_b, ()), "x", "y")
    kv_a, kv_b, kv_zero, states_a, states_b = join_four(
        (near_a, one_a, three_a, low_a, high_a), (near_b, one_b, three_b, low_b, high_b), ()
    )
    mask_two = retrieval_mask(place, retrieved, 1, (kv_a,))
    bias = (mask_one, mask_two)
    far_zero = shift(kv_zero, "core", 1)
    one_a, three_a = neighbours(kv_a, "y")
    one_b, three_b = neighbours(kv_b, "x")
    cut = halve(one_a, three_a, one_b, three_b, (mask_two,))
    low_a, high_a, low_b, high_b = pass_on(cut, "y", "x")

    h_one, normed_one, inv_one = layer_norm(
        x_in.astype(WIDE) + tensor_total(part), ln1_gain, ln1_bias
    )
    h_one_low = h_one.astype(LOW)
    q_cross = dot(h_one_low, cross_wq).astype(LOW) * jnp.asarray(SCALE, LOW)
    qt_cross = q_cross.T
    one_block = (((0, 0, 1024, 0),),)
    two_blocks = (((0, 0, 1024, 0),), ((0, 1024, 1024, 0),))
    state = cross_fwd(
        qt_cross,
        bias,
        (0, 4),
        (((0, 0, 1024, 0),), ((1, 0, 1024, 0),)),
        (kv_zero, far_zero),
        after=(cut[0],),
    )
    *state, kv_sides = cross_fwd(
        qt_cross,
        bias,
        (1, 3),
        (((0, 0, 512, 0), (1, 0, 512, 512)), ((2, 0, 512, 0), (3, 0, 512, 512))),
        (one_a, one_b, three_a, three_b),
        state,
        collect=True,
        after=(low_a, high_a, low_b, high_b),
    )
    far_sides = shift(kv_sides, "core", 1)
    *state, kv_two = cross_fwd(
        qt_cross,
        bias,
        (2,),
        (((0, 0, 256, 0), (1, 0, 256, 256), (2, 0, 256, 512), (3, 0, 256, 768)),),
        (low_a, high_a, low_b, high_b),
        state,
        collect=True,
    )
    far_two = shift(kv_two, "core", 1)
    state = cross_fwd(qt_cross, bias, (5, 7), two_blocks, (far_sides,), state)
    mixt_cross, mix_cross, lse_cross = cross_fwd(
        qt_cross, bias, (6,), one_block, (far_two,), state, last=True
    )
    h_two, normed_two, inv_two = layer_norm(
        h_one + tensor_total(dot(mix_cross, cross_wo)), ln2_gain, ln2_bias
    )
    h_two_low = h_two.astype(LOW)
    pre_act = dot(h_two_low, ffn_w1)
    act_low = jax.nn.gelu(pre_act).astype(LOW)
    h_three, normed_three, inv_three = layer_norm(
        h_two + tensor_total(dot(act_low, ffn_w2)), ln3_gain, ln3_bias
    )
    row_valid = (positions < lengths[0]).astype(WIDE)[:, None]
    block_out = (h_three * row_valid).astype(LOW)

    grad_out = cotangent.astype(WIDE) * row_valid
    d_three, grad_g3, grad_b3 = norm_back(grad_out, normed_three, inv_three, ln3_gain)
    e_three = d_three.astype(LOW)
    d_act = dot(e_three, ffn_w2, 1, 1)
    unused, gelu_back = jax.vjp(jax.nn.gelu, pre_act)
    d_pre = gelu_back(d_act)[0].astype(LOW)
    ffn_part = dot(d_pre, ffn_w1, 1, 1).astype(LOW)
    early_mine, early_theirs = ffn_grads(place, h_two_low, d_pre, e_three, act_low, (ffn_part,))
    early_got = shift(early_theirs, "core", 1)

    d_two, e_two, grad_g2, grad_b2 = norm_back_total(
        ffn_part, other_tensor(ffn_part), d_three, normed_two, inv_two, ln2_gain
    )
    dm_cross = dot(e_two, cross_wo, 1, 1).astype(LOW)
    dmt_cross = dm_cross.T
    inner = jnp.sum((dmt_cross.astype(WIDE) * mixt_cross).reshape(6, HEAD_DIM, tokens), axis=1)
    inner = jnp.concatenate([inner, jnp.zeros((2, tokens), WIDE)], axis=0)
    sides = (qt_cross, q_cross, dmt_cross, dm_cross, lse_cross, inner)

    dqt, far = cross_bwd(
        sides,
        jnp.zeros((384, tokens), WIDE),
        bias,
        (6, 5),
        (((0, 0, 1024, 0),), ((1, 0, 1024, 0),)),
        (far_two, far_sides),
        ((0, 0, 2048),),
    )
    early = early_first(place, early_mine, early_got, (dqt,))
    got_two_one = shift(far, "core", 1)
    dqt, far = cross_bwd(
        sides,
        dqt,
        bias,
        (7, 4),
        (((0, 1024, 1024, 0),), ((1, 0, 1024, 0),)),
        (far_sides, far_zero),
        ((0, 0, 2048),),
        after=(early[1],),
    )
    near_sums, early_yx = ring_halves(early, (dqt,))
    got_three_zero = shift(far, "core", 1)
    dqt, low_a, high_a, low_b, high_b = cross_bwd(
        sides,
        dqt,
        bias,
        (2,),
        one_block,
        (kv_two,),
        tuple((0, k * 256, 256) for k in range(4)),
        adds=one_block,
        add_arrays=(got_two_one,),
        after=(near_sums[0],),
    )
    low_a, low_b = shift(low_a, "y", -1), shift(low_b, "x", -1)
    high_a, high_b = shift(high_a, "y", 1), shift(high_b, "x", 1)
    dqt, own_a, own_b = cross_bwd(
        sides,
        dqt,
        bias,
        (0,),
        one_block,
        (kv_zero,),
        ((0, 0, 512), (0, 512, 512)),
        adds=(((0, 1024, 1024, 0),),),
        add_arrays=(got_three_zero,),
        after=(*early_yx[0], *early_yx[1]),
    )
    dqt, one_a, one_b, three_a, three_b = cross_bwd(
        sides,
        dqt,
        bias,
        (1, 3),
        two_blocks,
        (kv_sides,),
        ((0, 0, 512), (0, 512, 512), (1, 0, 512), (1, 512, 512)),
        adds=(((0, 1024, 1024, 0),), ((1, 0, 1024, 0),)),
        add_arrays=(got_two_one, got_three_zero),
        halves=(((0, 0, 256, 0), (1, 0, 256, 256)), ((2, 0, 256, 0), (3, 0, 256, 256))),
        half_arrays=(low_a, low_b, high_a, high_b),
    )
    got_a = [shift(one_a, "y", -1), shift(three_a, "y", 1)]
    got_b = [shift(one_b, "x", -1), shift(three_b, "x", 1)]

    blocks = store_sum_far((own_a, own_b), (got_a, got_b))
    got_a, got_b = returns(blocks[1:4], "x"), returns(blocks[5:8], "y")

    dqt_low = (dqt * SCALE).astype(LOW)
    query_part = dot(dqt_low, cross_wq, 0, 1).astype(LOW)
    d_one, e_one, grad_g1, grad_b1 = norm_back_total(
        query_part, other_tensor(query_part), d_two, normed_one, inv_one, ln1_gain
    )
    dq_self, dk_self, dv_self, part = self_bwd(
        e_one,
        q_self,
        k_self,
        v_self,
        mixt_self,
        lse_self,
        self_wq,
        self_wk,
        self_wv,
        self_wo,
        (blocks[1],),
    )
    part_got = other_tensor(part)
    input_grad = d_one + (part.astype(WIDE) + part_got.astype(WIDE))
    vectors = jnp.stack([grad_g1, grad_b1, grad_g2, grad_b2, grad_g3, grad_b3], axis=1)
    grads = [
        dot(x_in, dq_self, 0, 0),
        dot(x_in, dk_self, 0, 0),
        dot(x_in, dv_self, 0, 0),
        dot(e_one, mix_self, 0, 0),
        dot(h_one_low, dqt_low, 0, 1),
        dot(e_two, mix_cross, 0, 0),
        jnp.pad(vectors, ((0, 0), (0, 250))),
    ]
    grads = jnp.concatenate([g.astype(LOW) for g in grads], axis=1)
    late_got = to_other_core(grads)

    store_keep, store_give = store_weight_grads(place, (states_a, states_b), blocks)
    by_z = store_sum_mid((blocks[0], blocks[4]), (got_a, got_b))
    pieces = [by_z[0]] + returns(by_z[1:], "z")
    store_mine, store_send = store_finish(tensor_at, pieces, cross_wk, cross_wv)
    datastore_grad = store_mine + other_tensor(store_send).astype(WIDE)
    late = late_first(
        place, grads, late_got, store_keep, shift(store_give, "core", 1), (by_z[1],)
    )
    late_sums, late_yx = ring_halves(late)

    groups = (
        (0, late[0], late_yx[0]),
        (0, early[0], early_yx[0]),
        (1, late[5], late_yx[1]),
        (1, early[5], early_yx[1]),
    )
    blocks = weights_second(place, groups, ())
    late_xy = (returns(blocks[1:4], "x"), returns(blocks[5:8], "y"))
    last = weights_third(place, (blocks[0], blocks[4]), late_xy, (part_got,))
    keep, send = weights_fourth(place, last[0], returns(last[1:], "z"))
    got = shift(send, "core", 1).astype(WIDE)
    first = coord("core") == 0
    parts = (jnp.where(first, keep, got), jnp.where(first, got, keep))
    late_sum = jnp.concatenate(
        [c for h in parts for c in (h[:, :768], h[:, 1536:2048])], axis=1
    )
    store_sum = jnp.concatenate([h[:, 2048:2432] for h in parts], axis=1)
    grad_w1, grad_w2 = [jnp.concatenate([h[:, 768:1536], h[:, 2432:]], axis=1) for h in parts]

    part_of = lambda k: late_sum[:, k * 384 : (k + 1) * 384]
    vector = lambda k: late_sum[:, 2304 + k]
    return (
        block_out,
        input_grad,
        datastore_grad,
        part_of(0),
        part_of(1),
        part_of(2),
        part_of(3).T,
        vector(0),
        vector(1),
        part_of(4),
        store_sum[:, :384],
        store_sum[:, 384:],
        part_of(5).T,
        vector(2),
        vector(3),
        grad_w1,
        grad_w2.T,
        vector(4),
        vector(5),
    )


def solution(mesh):
    rows, columns, split = P("dp", None), P(None, "tensor"), P("tensor", None)
    norm = (P(), P())
    in_specs = (
        (rows, P("dp"), rows, rows)
        + (columns, columns, columns, split)
        + norm
        + (columns, columns, columns, split)
        + norm
        + (columns, split)
        + norm
        + (rows,)
    )
    both, turned, vector = P("dp", "tensor"), P("tensor", "dp"), P("dp")
    out_specs = (
        (rows, rows, both)
        + (both, both, both, turned)
        + (vector, vector)
        + (both, both, both, turned)
        + (vector, vector)
        + (both, turned)
        + (vector, vector)
    )
    return jax.shard_map(shards, mesh=mesh, in_specs=in_specs, out_specs=out_specs, check_vma=False)
```
